512 devices in a mesh: chan: 16 (over y, core), pix: 32 (over x, z).
Axes of the slice: x: 4, y: 8, z: 8, core: 2. Of those that a mesh axis runs over, the one named last changes fastest.
Arguments:
- cubes: float32 [2, 512, 262144], P(None, 'chan', 'pix'), may hold values from -4000 to 4000
- start_block: float32 [2, 512, 8], replicated, may hold values from -6 to 6
Outputs:
- spectrum: float32 [2, 2, 256, 262144], P(None, None, 'chan', 'pix')
The draws below stay inside these ranges and needn't reach their ends.
All inputs are finite; a program needn't handle non-finite values.
Results may differ from the reference program's by a relative error of at most 0.0003.
Values sent between devices are 32-bit elements; how exact they have to be, the bound alone decides.
No kernel may reach another device: no remote copies, remote signals or barrier semaphores. Data moves between devices by JAX's collectives and lax.ppermute only.
A program may use at most 64 MiB of HBM per device.

```python
import jax
import jax.numpy as jnp
from jax import lax

F = 512
MODES = 8
ITERS = 2
SPECIES = 2
K = 256
NPIX = 262144


def draw_cubes(key, part):
    key = jax.random.fold_in(key, 11)
    keys = jax.random.split(key, 4)
    components = 12
    spectra = jax.random.normal(keys[0], (SPECIES, components, F), jnp.float32)
    maps = jax.random.normal(keys[1], (SPECIES, components, NPIX), jnp.float32)
    chan_scale = jnp.exp(jax.random.uniform(keys[2], (SPECIES, F, 1), jnp.float32, 0.0, jnp.log(10.0)))
    ramp = 1.0 + 2.0 * jnp.arange(NPIX, dtype=jnp.float32) / NPIX
    noise = 0.4 * jax.random.normal(keys[3], (SPECIES, F, NPIX), jnp.float32)
    decay = 0.88
    total = noise
    for comp in range(components):
        total = total + decay ** comp * spectra[:, comp, :, None] * maps[:, comp, None, :]
    return (total * chan_scale * ramp[None, None, :]).astype(jnp.float32)


def scatter_about(own_key, dims, scale, limit, held_as=jnp.bfloat16):
    drawn = jax.random.normal(own_key, dims, jnp.float32) * scale
    return jnp.minimum(jnp.maximum(drawn, -limit), limit).astype(held_as)


def setup_inputs(seed: int = 0) -> dict:
    key_list = jax.random.split(jax.random.key(seed), 3)
    cubes = draw_cubes(jax.random.fold_in(key_list[2], 71), 0)
    start_block = scatter_about(key_list[1], (SPECIES, F, MODES), 1.0, 6.0, jnp.float32)
    return {"cubes": cubes, "start_block": start_block}


HP = lax.Precision.HIGHEST

def orthonormal(grown):
    inner = jnp.einsum('sfm,sfn->smn', grown, grown, precision=HP)
    lower = jnp.linalg.cholesky(inner)
    return lax.linalg.triangular_solve(lower, grown, left_side=False, lower=True, transpose_a=True)

def tables(count, width):
    rows = jnp.arange(count, dtype=jnp.int32)[:, None]
    cols = jnp.arange(width, dtype=jnp.int32)[None, :]
    phase = (rows * cols % width).astype(jnp.float32) * (2.0 * jnp.pi / width)
    norm = 1.0 / jnp.sqrt(jnp.float32(width))
    return (jnp.cos(phase) * norm, jnp.sin(phase) * norm)

def reference(cubes, start_block):
    total = cubes.shape[2]
    cov = jnp.einsum('sfp,sgp->sfg', cubes, cubes, precision=HP) / total
    basis = start_block
    for step in range(ITERS):
        grown = jnp.einsum('sfg,sgm->sfm', cov, basis, precision=HP)
        basis = orthonormal(grown)
    weights = jnp.einsum('sfm,sfp->smp', basis, cubes, precision=HP)
    cleaned = cubes - jnp.einsum('sfm,smp->sfp', basis, weights, precision=HP)
    cosine, sine = tables(K, F)
    real_part = jnp.einsum('kf,sfp->skp', cosine, cleaned, precision=HP)
    imag_part = -jnp.einsum('kf,sfp->skp', sine, cleaned, precision=HP)
    return jnp.stack([real_part, imag_part])
```

```python
import jax
import jax.numpy as jnp
import numpy as np
from jax import lax
from jax.experimental import pallas as pl
from jax.experimental.pallas import tpu as pltpu
from jax.sharding import PartitionSpec as P

ITERS = 2
LANES = 128
HP = lax.Precision.HIGHEST
VMEM = pl.BlockSpec(memory_space=pltpu.VMEM)
ANY = pl.BlockSpec(memory_space=pl.ANY)
PARAMS = pltpu.CompilerParams(vmem_limit_bytes=40 * 1024 * 1024)


def swap(value, axis):
    return lax.all_to_all(value, axis, split_axis=0, concat_axis=0, tiled=True)


def to_all(value, axis):
    count = lax.axis_size(axis)
    return swap(jnp.broadcast_to(value[None], (count,) + value.shape), axis)


def split_pixels(cubes, parts):
    species, chans, pixels = cubes.shape
    step = pixels // parts

    def kernel(src, dst, sems):
        copies = [
            pltpu.make_async_copy(src.at[:, :, pl.ds(j * step, step)], dst.at[j], sems.at[j])
            for j in range(parts)
        ]
        for copy in copies:
            copy.start()
        for copy in copies:
            copy.wait()

    return pl.pallas_call(
        kernel,
        out_shape=jax.ShapeDtypeStruct((parts, species, chans, step), cubes.dtype),
        in_specs=[ANY],
        out_specs=ANY,
        scratch_shapes=[pltpu.SemaphoreType.DMA((parts,))],
    )(cubes)


def join_pixels(blocks):
    parts, halves, species, waves, step = blocks.shape

    def kernel(src, dst, sems):
        copies = [
            pltpu.make_async_copy(src.at[j], dst.at[:, :, :, pl.ds(j * step, step)], sems.at[j])
            for j in range(parts)
        ]
        for copy in copies:
            copy.start()
        for copy in copies:
            copy.wait()

    return pl.pallas_call(
        kernel,
        out_shape=jax.ShapeDtypeStruct((halves, species, waves, parts * step), blocks.dtype),
        in_specs=[ANY],
        out_specs=ANY,
        scratch_shapes=[pltpu.SemaphoreType.DMA((parts,))],
    )(blocks)


def dot(a, b, dims=((1,), (0,)), precision=HP):
    return lax.dot_general(a, b, (dims, ((), ())), precision=precision, preferred_element_type=jnp.float32)


def cube_of(x_ref, s):
    parts, _, chans, pixels = x_ref.shape
    return x_ref[:, s].reshape(parts * chans, pixels)


def grow(rows, x, scale, out_ref, s):
    modes = rows.shape[0]
    weights = dot(rows, x) * scale
    grown = dot(weights, x, ((1,), (1,)))
    for c in range(grown.shape[1] // LANES):
        out_ref[s * modes : (s + 1) * modes, c, :] = grown[:, c * LANES : (c + 1) * LANES]


def grown_rows(g_ref, s, modes):
    return jnp.concatenate([g_ref[s * modes : (s + 1) * modes, c, :] for c in range(g_ref.shape[1])], axis=1)


def orthonormal(rows):
    modes = rows.shape[0]
    index = lax.broadcasted_iota(jnp.int32, (modes, 1), 0)
    for j in range(modes - 1):
        pivot = rows[j : j + 1]
        prods = jnp.sum(rows * pivot, axis=1, keepdims=True)
        ratio = jnp.where(index > j, prods / prods[j : j + 1], 0.0)
        rows = rows - ratio * pivot
    norms = jnp.sum(rows * rows, axis=1, keepdims=True)
    inverse = lax.rsqrt(norms)
    inverse = inverse * (1.5 - 0.5 * norms * inverse * inverse)
    return rows * inverse


def first_kernel(scale, x_ref, start_ref, out_ref):
    for s in range(x_ref.shape[1]):
        grow(start_ref[s], cube_of(x_ref, s), scale, out_ref, s)


def next_kernel(scale, modes, x_ref, g_ref, out_ref):
    for s in range(x_ref.shape[1]):
        rows = orthonormal(grown_rows(g_ref, s, modes))
        grow(rows, cube_of(x_ref, s), scale, out_ref, s)


def parts_of(value, count):
    parts = []
    for _ in range(count):
        part = value.astype(jnp.bfloat16)
        parts.append(part)
        value = value - part.astype(jnp.float32)
    return parts


def last_kernel(modes, x_ref, g_ref, table_ref, out_ref):
    for s in range(x_ref.shape[1]):
        x = cube_of(x_ref, s)
        rows = orthonormal(grown_rows(g_ref, s, modes))
        weights = dot(rows, x)
        cleaned = x - dot(rows, weights, ((0,), (0,)))
        high, low = parts_of(cleaned, 2)
        stacked = jnp.concatenate([high, low, high], axis=0)
        spectrum = dot(table_ref[...], stacked, precision=None)
        out_ref[:, :, s] = spectrum.reshape(out_ref.shape[0], out_ref.shape[1], out_ref.shape[3], out_ref.shape[4])


def tables(owners, waves, width):
    k = np.arange(waves)[:, None]
    f = np.arange(width)[None, :]
    phase = 2.0 * np.pi * (k * f % width) / width
    both = np.stack([np.cos(phase), -np.sin(phase)]) / np.sqrt(width)
    rows = both.reshape(2, owners, waves // owners, width).transpose(1, 0, 2, 3).reshape(2 * waves, width)
    rows = rows.astype(np.float32)
    high = rows.astype(jnp.bfloat16)
    low = (rows - high.astype(np.float32)).astype(jnp.bfloat16)
    return np.concatenate([high, high, low], axis=1)


def body(cubes, start_block):
    owners = lax.axis_size("chan")
    species, chans, pixels = cubes.shape
    width = chans * owners
    modes = start_block.shape[2]
    waves = width // 2
    step = pixels // owners
    scale = 1.0 / (pixels * lax.axis_size("pix"))

    share = jax.ShapeDtypeStruct((species * modes, width // LANES, LANES), jnp.float32)

    def summed(part):
        row = jnp.sum(swap(part, "chan"), axis=0)
        row = jnp.sum(to_all(row, "pix"), axis=0)
        return to_all(row, "chan")

    x = swap(split_pixels(cubes, owners), "chan")
    grown = pl.pallas_call(
        lambda *refs: first_kernel(scale, *refs),
        out_shape=share, in_specs=[VMEM, VMEM], out_specs=VMEM, compiler_params=PARAMS,
    )(x, jnp.swapaxes(start_block, 1, 2))
    grown = summed(grown)
    for _ in range(ITERS - 1):
        grown = pl.pallas_call(
            lambda *refs: next_kernel(scale, modes, *refs),
            out_shape=share, in_specs=[VMEM, VMEM], out_specs=VMEM, compiler_params=PARAMS,
        )(x, grown)
        grown = summed(grown)
    blocks = pl.pallas_call(
        lambda *refs: last_kernel(modes, *refs),
        out_shape=jax.ShapeDtypeStruct((owners, 2, species, waves // owners, step), jnp.float32),
        in_specs=[VMEM, VMEM, VMEM], out_specs=VMEM, compiler_params=PARAMS,
    )(x, grown, jnp.asarray(tables(owners, waves, width)))
    return join_pixels(swap(blocks, "chan"))


def solution(mesh):
    placed = (P(None, "chan", "pix"), P())
    return jax.shard_map(
        body, mesh=mesh, in_specs=placed, out_specs=P(None, None, "chan", "pix"), check_vma=False
    )
```

```python
import jax
import jax.numpy as jnp
import numpy as np
from jax import lax
from jax.experimental import pallas as pl
from jax.experimental.pallas import tpu as pltpu
from jax.sharding import PartitionSpec as P

ITERS = 2
LANES = 128
HP = lax.Precision.HIGHEST
VMEM = pl.BlockSpec(memory_space=pltpu.VMEM)
ANY = pl.BlockSpec(memory_space=pl.ANY)
PARAMS = pltpu.CompilerParams(vmem_limit_bytes=40 * 1024 * 1024)


def swap(value, axis):
    return lax.all_to_all(value, axis, split_axis=0, concat_axis=0, tiled=True)


def to_all(value, axis):
    count = lax.axis_size(axis)
    return swap(jnp.broadcast_to(value[None], (count,) + value.shape), axis)


def split_pixels(cubes, parts):
    species, chans, pixels = cubes.shape
    step = pixels // parts

    def kernel(src, dst, sems):
        copies = [
            pltpu.make_async_copy(src.at[:, :, pl.ds(j * step, step)], dst.at[j], sems.at[j])
            for j in range(parts)
        ]
        for copy in copies:
            copy.start()
        for copy in copies:
            copy.wait()

    return pl.pallas_call(
        kernel,
        out_shape=jax.ShapeDtypeStruct((parts, species, chans, step), cubes.dtype),
        in_specs=[ANY],
        out_specs=VMEM,
        scratch_shapes=[pltpu.SemaphoreType.DMA((parts,))],
    )(cubes)


def join_pixels(blocks):
    parts, halves, species, waves, step = blocks.shape

    def kernel(src, dst, sems):
        copies = [
            pltpu.make_async_copy(src.at[j], dst.at[:, :, :, pl.ds(j * step, step)], sems.at[j])
            for j in range(parts)
        ]
        for copy in copies:
            copy.start()
        for copy in copies:
            copy.wait()

    return pl.pallas_call(
        kernel,
        out_shape=jax.ShapeDtypeStruct((halves, species, waves, parts * step), blocks.dtype),
        in_specs=[VMEM],
        out_specs=ANY,
        scratch_shapes=[pltpu.SemaphoreType.DMA((parts,))],
    )(blocks)


def dot(a, b, dims=((1,), (0,)), precision=HP):
    return lax.dot_general(a, b, (dims, ((), ())), precision=precision, preferred_element_type=jnp.float32)


def cube_of(x_ref, s):
    parts, _, chans, pixels = x_ref.shape
    return x_ref[:, s].reshape(parts * chans, pixels)


def grow(rows, x, scale, out_ref, s):
    modes = rows.shape[0]
    weights = dot(rows, x) * scale
    grown = dot(weights, x, ((1,), (1,)))
    for c in range(grown.shape[1] // LANES):
        out_ref[s * modes : (s + 1) * modes, c, :] = grown[:, c * LANES : (c + 1) * LANES]


def grown_rows(g_ref, s, modes):
    return jnp.concatenate([g_ref[s * modes : (s + 1) * modes, c, :] for c in range(g_ref.shape[1])], axis=1)


def orthonormal(rows):
    modes = rows.shape[0]
    index = lax.broadcasted_iota(jnp.int32, (modes, 1), 0)
    for j in range(modes - 1):
        pivot = rows[j : j + 1]
        prods = jnp.sum(rows * pivot, axis=1, keepdims=True)
        ratio = jnp.where(index > j, prods / prods[j : j + 1], 0.0)
        rows = rows - ratio * pivot
    norms = jnp.sum(rows * rows, axis=1, keepdims=True)
    inverse = lax.rsqrt(norms)
    inverse = inverse * (1.5 - 0.5 * norms * inverse * inverse)
    return rows * inverse


def first_kernel(scale, x_ref, start_ref, out_ref):
    for s in range(x_ref.shape[1]):
        grow(start_ref[s], cube_of(x_ref, s), scale, out_ref, s)


def next_kernel(scale, modes, x_ref, g_ref, out_ref):
    for s in range(x_ref.shape[1]):
        rows = orthonormal(grown_rows(g_ref, s, modes))
        grow(rows, cube_of(x_ref, s), scale, out_ref, s)


def parts_of(value, count):
    parts = []
    for _ in range(count):
        part = value.astype(jnp.bfloat16)
        parts.append(part)
        value = value - part.astype(jnp.float32)
    return parts


def last_kernel(modes, x_ref, g_ref, table_ref, out_ref):
    for s in range(x_ref.shape[1]):
        x = cube_of(x_ref, s)
        rows = orthonormal(grown_rows(g_ref, s, modes))
        weights = dot(rows, x)
        cleaned = x - dot(rows, weights, ((0,), (0,)))
        high, low = parts_of(cleaned, 2)
        stacked = jnp.concatenate([high, low, high], axis=0)
        spectrum = dot(table_ref[...], stacked, precision=None)
        out_ref[:, :, s] = spectrum.reshape(out_ref.shape[0], out_ref.shape[1], out_ref.shape[3], out_ref.shape[4])


def tables(owners, waves, width):
    k = np.arange(waves)[:, None]
    f = np.arange(width)[None, :]
    phase = 2.0 * np.pi * (k * f % width) / width
    both = np.stack([np.cos(phase), -np.sin(phase)]) / np.sqrt(width)
    rows = both.reshape(2, owners, waves // owners, width).transpose(1, 0, 2, 3).reshape(2 * waves, width)
    rows = rows.astype(np.float32)
    high = rows.astype(jnp.bfloat16)
    low = (rows - high.astype(np.float32)).astype(jnp.bfloat16)
    return np.concatenate([high, high, low], axis=1)


def body(cubes, start_block):
    owners = lax.axis_size("chan")
    species, chans, pixels = cubes.shape
    width = chans * owners
    modes = start_block.shape[2]
    waves = width // 2
    step = pixels // owners
    scale = 1.0 / (pixels * lax.axis_size("pix"))

    share = jax.ShapeDtypeStruct((species * modes, width // LANES, LANES), jnp.float32)

    def summed(part):
        row = jnp.sum(swap(part, "chan"), axis=0)
        row = jnp.sum(to_all(row, "pix"), axis=0)
        return to_all(row, "chan")

    x = swap(split_pixels(cubes, owners), "chan")
    grown = pl.pallas_call(
        lambda *refs: first_kernel(scale, *refs),
        out_shape=share, in_specs=[VMEM, VMEM], out_specs=VMEM, compiler_params=PARAMS,
    )(x, jnp.swapaxes(start_block, 1, 2))
    grown = summed(grown)
    for _ in range(ITERS - 1):
        grown = pl.pallas_call(
            lambda *refs: next_kernel(scale, modes, *refs),
            out_shape=share, in_specs=[VMEM, VMEM], out_specs=VMEM, compiler_params=PARAMS,
        )(x, grown)
        grown = summed(grown)
    blocks = pl.pallas_call(
        lambda *refs: last_kernel(modes, *refs),
        out_shape=jax.ShapeDtypeStruct((owners, 2, species, waves // owners, step), jnp.float32),
        in_specs=[VMEM, VMEM, VMEM], out_specs=VMEM, compiler_params=PARAMS,
    )(x, grown, jnp.asarray(tables(owners, waves, width)))
    return join_pixels(swap(blocks, "chan"))


def solution(mesh):
    placed = (P(None, "chan", "pix"), P())
    return jax.shard_map(
        body, mesh=mesh, in_specs=placed, out_specs=P(None, None, "chan", "pix"), check_vma=False
    )
```

```python
import jax
import jax.numpy as jnp
import numpy as np
from jax import lax
from jax.experimental import pallas as pl
from jax.experimental.pallas import tpu as pltpu
from jax.sharding import PartitionSpec as P

ITERS = 2
LANES = 128
INNER, ROWS, OUTER = ((1,), (0,)), ((1,), (1,)), ((0,), (0,))
VMEM = pl.BlockSpec(memory_space=pltpu.VMEM)
HBM = pl.BlockSpec(memory_space=pltpu.HBM)
DMA = pltpu.SemaphoreType.DMA


def params(mib):
    return pltpu.CompilerParams(vmem_limit_bytes=mib * 1024 * 1024)


def swap(value, axis):
    return lax.all_to_all(value, axis, split_axis=0, concat_axis=0, tiled=True)


def to_all(value, axis):
    count = lax.axis_size(axis)
    return swap(jnp.broadcast_to(value[None], (count,) + value.shape), axis)


def shape(*dims):
    return jax.ShapeDtypeStruct(dims, jnp.float32)


def dot(a, b, dims):
    return lax.dot_general(a, b, (dims, ((), ())), preferred_element_type=jnp.float32)


def cube_of(x_ref, s):
    parts, _, chans, pixels = x_ref.shape
    return x_ref[:, s].reshape(parts * chans, pixels)


def parts_of(value, count):
    parts = []
    for _ in range(count):
        part = value.astype(jnp.bfloat16)
        parts.append(part)
        value = value - part.astype(jnp.float32)
    return parts


def split_kernel(src, dst):
    step = dst.shape[3]
    for j in range(dst.shape[0]):
        dst[j] = src[:, :, j * step : (j + 1) * step]


def products(rows, x_parts, dims):
    count = rows.shape[0]
    stacked = [part.astype(jnp.float32) for part in parts_of(rows, 3)]
    stacked = jnp.concatenate(stacked, axis=0).astype(jnp.bfloat16)
    a = dot(stacked, x_parts[0], dims)
    b = dot(stacked[: 2 * count], x_parts[1], dims)
    c = dot(stacked[:count], x_parts[2], dims)
    return a[:count] + ((a[count : 2 * count] + b[:count]) + ((a[2 * count :] + b[count:]) + c))


def expand(rows, weights):
    left = [part.astype(jnp.float32) for part in parts_of(rows, 3)]
    right = [part.astype(jnp.float32) for part in parts_of(weights, 3)]
    pairs = [(0, 0), (0, 1), (1, 0), (0, 2), (1, 1), (2, 0)]
    left = jnp.concatenate([left[a] for a, _ in pairs], axis=0).astype(jnp.bfloat16)
    right = jnp.concatenate([right[b] for _, b in pairs], axis=0).astype(jnp.bfloat16)
    return dot(left, right, OUTER)


def grow(rows, x, scale, out_ref, s):
    modes = rows.shape[0]
    x_parts = parts_of(x, 3)
    weights = products(rows, x_parts, INNER) * scale
    grown = products(weights, x_parts, ROWS)
    for c in range(grown.shape[1] // LANES):
        out_ref[s * modes : (s + 1) * modes, c, :] = grown[:, c * LANES : (c + 1) * LANES]


def grown_rows(g_ref, s, modes):
    return jnp.concatenate([g_ref[s * modes : (s + 1) * modes, c, :] for c in range(g_ref.shape[1])], axis=1)


def orthonormal(rows):
    modes = rows.shape[0]
    index = lax.broadcasted_iota(jnp.int32, (modes, 1), 0)
    for j in range(modes - 1):
        pivot = rows[j : j + 1]
        prods = jnp.sum(rows * pivot, axis=1, keepdims=True)
        ratio = jnp.where(index > j, prods / prods[j : j + 1], 0.0)
        rows = rows - ratio * pivot
    norms = jnp.sum(rows * rows, axis=1, keepdims=True)
    inverse = lax.rsqrt(norms)
    inverse = inverse * (1.5 - 0.5 * norms * inverse * inverse)
    return rows * inverse


def first_kernel(scale, x_ref, start_ref, out_ref):
    for s in range(x_ref.shape[1]):
        grow(start_ref[s], cube_of(x_ref, s), scale, out_ref, s)


def next_kernel(scale, modes, x_ref, g_ref, out_ref):
    for s in range(x_ref.shape[1]):
        rows = orthonormal(grown_rows(g_ref, s, modes))
        grow(rows, cube_of(x_ref, s), scale, out_ref, s)


def last_kernel(modes, x_ref, g_ref, table_ref, out_ref, held, sem):
    copy = pltpu.make_async_copy(table_ref, held, sem)
    copy.start()
    owners, halves, _, waves, step = out_ref.shape
    count = held.shape[0] // 2
    bases = [orthonormal(grown_rows(g_ref, s, modes)) for s in range(x_ref.shape[1])]
    for s, rows in enumerate(bases):
        x = cube_of(x_ref, s)
        weights = products(rows, parts_of(x, 3), INNER)
        high, low = parts_of(x - expand(rows, weights), 2)
        if s == 0:
            copy.wait()
        a = dot(held[...], high, INNER)
        total = a[:count] + (a[count:] + dot(held[:count], low, INNER))
        out_ref[:, :, s] = total.reshape(owners, halves, waves, step)


def join_kernel(src, dst, held, sems):
    parts, halves, species, _, step = src.shape
    copies = []
    for h in range(halves):
        for s in range(species):
            for j in range(parts):
                held[h, s, :, j * step : (j + 1) * step] = src[j, h, s]
            copy = pltpu.make_async_copy(held.at[h, s], dst.at[h, s], sems.at[h, s])
            copy.start()
            copies.append(copy)
    for copy in copies:
        copy.wait()


def tables(owners, waves, width):
    k = np.arange(waves)[:, None]
    f = np.arange(width)[None, :]
    phase = 2.0 * np.pi * (k * f % width) / width
    both = np.stack([np.cos(phase), -np.sin(phase)]) / np.sqrt(width)
    rows = both.reshape(2, owners, waves // owners, width).transpose(1, 0, 2, 3).reshape(2 * waves, width)
    high = rows.astype(jnp.bfloat16)
    low = (rows - high.astype(np.float64)).astype(jnp.bfloat16)
    return np.concatenate([high, low])


def body(cubes, start_block):
    owners = lax.axis_size("chan")
    species, chans, pixels = cubes.shape
    width = chans * owners
    modes = start_block.shape[2]
    waves = width // 2
    step = pixels // owners
    scale = 1.0 / (pixels * lax.axis_size("pix"))
    share = shape(species * modes, width // LANES, LANES)

    def summed(part):
        row = jnp.sum(swap(part, "chan"), axis=0)
        row = jnp.sum(to_all(row, "pix"), axis=0)
        return to_all(row, "chan")

    split = pl.pallas_call(
        split_kernel,
        out_shape=shape(owners, species, chans, step), in_specs=[VMEM], out_specs=VMEM, compiler_params=params(4),
    )(cubes)
    x = swap(split, "chan")
    grown = pl.pallas_call(
        lambda *refs: first_kernel(scale, *refs),
        out_shape=share, in_specs=[VMEM, VMEM], out_specs=VMEM, compiler_params=params(24),
    )(x, jnp.swapaxes(start_block, 1, 2))
    grown = summed(grown)
    for _ in range(ITERS - 1):
        grown = pl.pallas_call(
            lambda *refs: next_kernel(scale, modes, *refs),
            out_shape=share, in_specs=[VMEM, VMEM], out_specs=VMEM, compiler_params=params(24),
        )(x, grown)
        grown = summed(grown)
    blocks = pl.pallas_call(
        lambda *refs: last_kernel(modes, *refs),
        out_shape=shape(owners, 2, species, waves // owners, step),
        in_specs=[VMEM, VMEM, HBM], out_specs=VMEM, compiler_params=params(24),
        scratch_shapes=[pltpu.VMEM((4 * waves, width), jnp.bfloat16), DMA],
    )(x, grown, jnp.asarray(tables(owners, waves, width)))
    return pl.pallas_call(
        join_kernel,
        out_shape=shape(2, species, waves // owners, pixels), in_specs=[VMEM], out_specs=HBM, compiler_params=params(8),
        scratch_shapes=[pltpu.VMEM((2, species, waves // owners, pixels), jnp.float32), DMA((2, species))],
    )(swap(blocks, "chan"))


def solution(mesh):
    placed = (P(None, "chan", "pix"), P())
    return jax.shard_map(
        body, mesh=mesh, in_specs=placed, out_specs=P(None, None, "chan", "pix"), check_vma=False
    )
```

```python
import jax
import jax.numpy as jnp
import numpy as np
from jax import lax
from jax.experimental import pallas as pl
from jax.experimental.pallas import tpu as pltpu
from jax.sharding import PartitionSpec as P

ITERS = 2
LANES = 128
GROUPS = 4
INNER, ROWS, OUTER = ((1,), (0,)), ((1,), (1,)), ((0,), (0,))
VMEM = pl.BlockSpec(memory_space=pltpu.VMEM)
HBM = pl.BlockSpec(memory_space=pltpu.HBM)
DMA = pltpu.SemaphoreType.DMA


def params(mib):
    return pltpu.CompilerParams(vmem_limit_bytes=mib * 1024 * 1024)


def swap(value, axis):
    return lax.all_to_all(value, axis, split_axis=0, concat_axis=0, tiled=True)


def to_all(value, axis):
    count = lax.axis_size(axis)
    return swap(jnp.broadcast_to(value[None], (count,) + value.shape), axis)


def after(value, others):
    return lax.optimization_barrier((value, others))


def cost(flops, moved):
    return pl.CostEstimate(flops=flops, bytes_accessed=moved, transcendentals=0)


def shape(*dims):
    return jax.ShapeDtypeStruct(dims, jnp.float32)


def dot(a, b, dims):
    return lax.dot_general(a, b, (dims, ((), ())), preferred_element_type=jnp.float32)


def cube_of(x_ref, s):
    parts, _, chans, pixels = x_ref.shape
    return x_ref[:, s].reshape(parts * chans, pixels)


def turned_cube(x_ref, s):
    owners, _, rows, pixels = x_ref.shape
    step = rows // GROUPS
    groups = [x_ref[:, s, q * step : (q + 1) * step].reshape(owners * step, pixels) for q in range(GROUPS)]
    return jnp.concatenate(groups, axis=0)


def store_turned(out_ref, value, s):
    owners, _, rows, pixels = out_ref.shape
    step = rows // GROUPS
    for q in range(GROUPS):
        part = value[q * owners * step : (q + 1) * owners * step]
        out_ref[:, s, q * step : (q + 1) * step] = part.reshape(owners, step, pixels)


def folded(value, axis):
    half = value.shape[axis] // 2
    first, second = lax.slice_in_dim(value, 0, half, axis=axis), lax.slice_in_dim(value, half, 2 * half, axis=axis)
    return first + second, first - second


def parts_of(value, count):
    parts = []
    for _ in range(count):
        part = value.astype(jnp.bfloat16)
        parts.append(part)
        value = value - part.astype(jnp.float32)
    return parts


def split_kernel(src, dst):
    step = dst.shape[3]
    for j in range(dst.shape[0]):
        dst[j] = src[:, :, j * step : (j + 1) * step]


def products_of_parts(left, right, dims):
    count = left[0].shape[0]
    stacked = jnp.concatenate(left, axis=0)
    a = dot(stacked, right[0], dims)
    b = dot(stacked[: 2 * count], right[1], dims)
    c = dot(stacked[:count], right[2], dims)
    return a[:count] + ((a[count : 2 * count] + b[:count]) + ((a[2 * count :] + b[count:]) + c))


def products(rows, right, dims):
    count = rows.shape[0]
    stacked = jnp.concatenate([part.astype(jnp.float32) for part in parts_of(rows, 3)], axis=0).astype(jnp.bfloat16)
    a = dot(stacked, right[0], dims)
    b = dot(stacked[: 2 * count], right[1], dims)
    c = dot(stacked[:count], right[2], dims)
    return a[:count] + ((a[count : 2 * count] + b[:count]) + ((a[2 * count :] + b[count:]) + c))


def expand(rows, weights):
    left = [part.astype(jnp.float32) for part in parts_of(rows, 3)]
    right = [part.astype(jnp.float32) for part in parts_of(weights, 3)]
    pairs = [(0, 0), (0, 1), (1, 0), (0, 2), (1, 1), (2, 0)]
    left = jnp.concatenate([left[a] for a, _ in pairs], axis=0).astype(jnp.bfloat16)
    right = jnp.concatenate([right[b] for _, b in pairs], axis=0).astype(jnp.bfloat16)
    return dot(left, right, OUTER)


def store_rows(out_ref, rows, s):
    modes = rows.shape[0]
    for c in range(rows.shape[1] // LANES):
        out_ref[s * modes : (s + 1) * modes, c, :] = rows[:, c * LANES : (c + 1) * LANES]


def grown_rows(g_ref, s, modes):
    return jnp.concatenate([g_ref[s * modes : (s + 1) * modes, c, :] for c in range(g_ref.shape[1])], axis=1)


def inverse_factor(rows):
    modes = rows.shape[0]
    index = lax.broadcasted_iota(jnp.int32, (modes, 1), 0)
    taken = lax.broadcasted_iota(jnp.int32, (modes, LANES), 0) == lax.broadcasted_iota(jnp.int32, (modes, LANES), 1)
    taken = taken.astype(jnp.float32)
    for j in range(modes - 1):
        pivot = rows[j : j + 1]
        prods = jnp.sum(rows * pivot, axis=1, keepdims=True)
        ratio = jnp.where(index > j, prods / prods[j : j + 1], 0.0)
        rows = rows - ratio * pivot
        taken = taken - ratio * taken[j : j + 1]
    norms = jnp.sum(rows * rows, axis=1, keepdims=True)
    inverse = lax.rsqrt(norms)
    inverse = inverse * (1.5 - 0.5 * norms * inverse * inverse)
    return taken * inverse


def mixed(factor, rows):
    total = factor[:, 0:1] * rows[0:1]
    for j in range(1, rows.shape[0]):
        total = total + factor[:, j : j + 1] * rows[j : j + 1]
    return total


def first_kernel(scale, x_ref, start_ref, table_ref, out_ref):
    grown = []
    for s in range(x_ref.shape[1]):
        x_parts = parts_of(cube_of(x_ref, s), 3)
        weights = products(start_ref[s], x_parts, INNER) * scale
        grown.append(products(weights, x_parts, ROWS))
    turned = [
        products(rows, [table_ref[p, parity] for p in range(3)], ROWS)
        for parity, rows in enumerate(folded(jnp.concatenate(grown, axis=0), 1))
    ]
    half = turned[0].shape[1] // 2
    turned = [turned[q % 2][:, q // 2 * half : (q // 2 + 1) * half] for q in range(GROUPS)]
    store_rows(out_ref, jnp.concatenate(turned, axis=1), 0)


def transform_kernel(x_ref, table_ref, out_ref):
    for s in range(x_ref.shape[1]):
        halves = []
        for parity, x in enumerate(folded(cube_of(x_ref, s), 0)):
            halves.append(products_of_parts([table_ref[p, parity] for p in range(3)], parts_of(x, 3), INNER))
        half = halves[0].shape[0] // 2
        turned = [halves[q % 2][q // 2 * half : (q // 2 + 1) * half] for q in range(GROUPS)]
        store_turned(out_ref, jnp.concatenate(turned, axis=0), s)


def next_kernel(scale, modes, x_ref, g_ref, out_ref):
    species = range(x_ref.shape[1])
    grown = [grown_rows(g_ref, s, modes) for s in species]
    x_parts = [parts_of(turned_cube(x_ref, s), 3) for s in species]
    raised = [products(rows, parts, INNER) for rows, parts in zip(grown, x_parts)]
    factors = [inverse_factor(rows) for rows in grown]
    for s in species:
        store_rows(out_ref, products(mixed(factors[s], raised[s]) * scale, x_parts[s], ROWS), s)


def last_kernel(modes, x_ref, g_ref, out_ref):
    owners, _, tiles, rows, _ = out_ref.shape
    count = rows // GROUPS
    species = range(x_ref.shape[1])
    grown = [grown_rows(g_ref, s, modes) for s in species]
    cubes = [turned_cube(x_ref, s) for s in species]
    raised = [products(rows, parts_of(x, 3), INNER) for x, rows in zip(cubes, grown)]
    factors = [inverse_factor(rows) for rows in grown]
    for s in species:
        fix = expand(mixed(factors[s], grown[s]), mixed(factors[s], raised[s]))
        cleaned = cubes[s] - fix
        scaled = cleaned * np.float32(np.sqrt(0.5))
        for q in range(GROUPS):
            rows = pl.ds(q // 2 * count * 2 + q % 2, count, stride=2)
            for c in range(tiles):
                part = scaled[q * owners * count : (q + 1) * owners * count, c * LANES : (c + 1) * LANES]
                out_ref[:, s, c, rows, :] = part.reshape(owners, count, LANES)
        for c in range(tiles):
            out_ref[0, s, c, 0:1, :] = cleaned[0:1, c * LANES : (c + 1) * LANES]
            out_ref[0, s, c, 2 * count : 2 * count + 1, :] = jnp.zeros((1, LANES), jnp.float32)


def join_kernel(src, dst, held, sems):
    halves, species, waves, _ = dst.shape
    copies = []
    for h in range(halves):
        for s in range(species):
            for j in range(src.shape[0]):
                for c in range(src.shape[2]):
                    at = (j * src.shape[2] + c) * LANES
                    held[h, s, :, at : at + LANES] = src[j, s, c, h * waves : (h + 1) * waves]
            copy = pltpu.make_async_copy(held.at[h, s], dst.at[h, s], sems.at[h, s])
            copy.start()
            copies.append(copy)
    for copy in copies:
        copy.wait()


def tables(owners, waves, width):
    k = np.arange(waves)[:, None]
    f = np.arange(width // 2)[None, :]
    phase = 2.0 * np.pi * (k * f % width) / width
    both = np.stack([np.cos(phase), -np.sin(phase)]) * np.sqrt(2.0 / width)
    both[0, 0] = 1.0 / np.sqrt(width)
    both[1, 0] = (1.0 - 2.0 * (f[0] % 2)) / np.sqrt(width)
    left = both.reshape(2, owners, waves // owners // 2, 2, width // 2).transpose(3, 0, 1, 2, 4).reshape(2, waves, width // 2)
    parts = []
    for _ in range(3):
        part = left.astype(jnp.bfloat16)
        parts.append(part)
        left = left - part.astype(np.float64)
    return np.stack(parts)


def body(cubes, start_block):
    owners = lax.axis_size("chan")
    species, chans, pixels = cubes.shape
    width = chans * owners
    modes = start_block.shape[2]
    waves = width // 2
    step = pixels // owners
    scale = 1.0 / (pixels * lax.axis_size("pix"))
    share = shape(species * modes, width // LANES, LANES)
    split_shape = shape(owners, species, chans, step)
    table = jnp.asarray(tables(owners, waves, width))
    work = 2 * species * width * step
    grant = params(24)

    split = pl.pallas_call(
        split_kernel,
        out_shape=split_shape, in_specs=[VMEM], out_specs=VMEM, compiler_params=params(4),
    )(cubes)
    x = swap(split, "chan")
    part = pl.pallas_call(
        lambda *refs: first_kernel(scale, *refs),
        out_shape=share, in_specs=[VMEM, VMEM, VMEM], out_specs=VMEM, compiler_params=grant,
        cost_estimate=cost(12 * modes * work, work),
    )(x, jnp.swapaxes(start_block, 1, 2), table)

    row = jnp.sum(swap(part, "chan"), axis=0)
    row, given = after(row, x)
    x = pl.pallas_call(
        transform_kernel,
        out_shape=split_shape, in_specs=[VMEM, VMEM], out_specs=VMEM, input_output_aliases={0: 0},
        compiler_params=grant, cost_estimate=cost(6 * waves * work, 6 * work),
    )(given, table)
    row = jnp.sum(to_all(row, "pix"), axis=0)
    row, x = after(row, x)
    grown = to_all(row, "chan")
    for _ in range(ITERS - 1):
        part = pl.pallas_call(
            lambda *refs: next_kernel(scale, modes, *refs),
            out_shape=share, in_specs=[VMEM, VMEM], out_specs=VMEM, compiler_params=grant,
        )(x, grown)
        row = jnp.sum(swap(part, "chan"), axis=0)
        row = jnp.sum(to_all(row, "pix"), axis=0)
        grown = to_all(row, "chan")
    blocks = pl.pallas_call(
        lambda *refs: last_kernel(modes, *refs),
        out_shape=shape(owners, species, step // LANES, chans, LANES), in_specs=[VMEM, VMEM], out_specs=VMEM, compiler_params=grant,
    )(x, grown)
    return pl.pallas_call(
        join_kernel,
        out_shape=shape(2, species, waves // owners, pixels), in_specs=[VMEM], out_specs=HBM, compiler_params=params(8),
        scratch_shapes=[pltpu.VMEM((2, species, waves // owners, pixels), jnp.float32), DMA((2, species))],
    )(swap(blocks, "chan"))


def solution(mesh):
    placed = (P(None, "chan", "pix"), P())
    return jax.shard_map(
        body, mesh=mesh, in_specs=placed, out_specs=P(None, None, "chan", "pix"), check_vma=False
    )
```

```python
import jax
import jax.numpy as jnp
import numpy as np
from jax import lax
from jax.experimental import pallas as pl
from jax.experimental.pallas import tpu as pltpu
from jax.sharding import PartitionSpec as P

LANES = 128
GROUPS = 4
INNER, ROWS, OUTER = ((1,), (0,)), ((1,), (1,)), ((0,), (0,))
VMEM = pl.BlockSpec(memory_space=pltpu.VMEM)
HBM = pl.BlockSpec(memory_space=pltpu.HBM)
DMA = pltpu.SemaphoreType.DMA


def params(mib):
    return pltpu.CompilerParams(vmem_limit_bytes=mib * 1024 * 1024)


def swap(value, axis):
    return lax.all_to_all(value, axis, split_axis=0, concat_axis=0, tiled=True)


def to_all(value, axis):
    count = lax.axis_size(axis)
    return swap(jnp.broadcast_to(value[None], (count,) + value.shape), axis)


def after(value, others):
    return lax.optimization_barrier((value, others))


def cost(flops, moved):
    return pl.CostEstimate(flops=flops, bytes_accessed=moved, transcendentals=0)


def shape(*dims):
    return jax.ShapeDtypeStruct(dims, jnp.float32)


def dot(a, b, dims):
    return lax.dot_general(a, b, (dims, ((), ())), preferred_element_type=jnp.float32)


def cube_of(x_ref, s):
    parts, _, chans, pixels = x_ref.shape
    return x_ref[:, s].reshape(parts * chans, pixels)


def turned_cube(x_ref, s):
    owners, _, rows, pixels = x_ref.shape
    step = rows // GROUPS
    groups = [x_ref[:, s, q * step : (q + 1) * step].reshape(owners * step, pixels) for q in range(GROUPS)]
    return jnp.concatenate(groups, axis=0)


def store_turned(out_ref, value, s):
    owners, _, rows, pixels = out_ref.shape
    step = rows // GROUPS
    for q in range(GROUPS):
        part = value[q * owners * step : (q + 1) * owners * step]
        out_ref[:, s, q * step : (q + 1) * step] = part.reshape(owners, step, pixels)


def folded(value, axis):
    half = value.shape[axis] // 2
    first, second = lax.slice_in_dim(value, 0, half, axis=axis), lax.slice_in_dim(value, half, 2 * half, axis=axis)
    return first + second, first - second


def parts_of(value, count):
    parts = []
    for _ in range(count):
        part = value.astype(jnp.bfloat16)
        parts.append(part)
        value = value - part.astype(jnp.float32)
    return parts


def split_kernel(src, dst):
    step = dst.shape[3]
    for j in range(dst.shape[0]):
        dst[j] = src[:, :, j * step : (j + 1) * step]


def products_of_parts(left, right, dims):
    count = left[0].shape[0]
    stacked = jnp.concatenate(left, axis=0)
    a = dot(stacked, right[0], dims)
    b = dot(stacked[: 2 * count], right[1], dims)
    c = dot(stacked[:count], right[2], dims)
    return a[:count] + ((a[count : 2 * count] + b[:count]) + ((a[2 * count :] + b[count:]) + c))


def products(rows, right, dims):
    count = rows.shape[0]
    stacked = jnp.concatenate([part.astype(jnp.float32) for part in parts_of(rows, 3)], axis=0).astype(jnp.bfloat16)
    a = dot(stacked, right[0], dims)
    b = dot(stacked[: 2 * count], right[1], dims)
    c = dot(stacked[:count], right[2], dims)
    return a[:count] + ((a[count : 2 * count] + b[:count]) + ((a[2 * count :] + b[count:]) + c))


def expand(rows, weights):
    left = [part.astype(jnp.float32) for part in parts_of(rows, 3)]
    right = [part.astype(jnp.float32) for part in parts_of(weights, 3)]
    pairs = [(0, 0), (0, 1), (1, 0), (0, 2), (1, 1), (2, 0)]
    left = jnp.concatenate([left[a] for a, _ in pairs], axis=0).astype(jnp.bfloat16)
    right = jnp.concatenate([right[b] for _, b in pairs], axis=0).astype(jnp.bfloat16)
    return dot(left, right, OUTER)


def store_rows(out_ref, rows, s):
    modes = rows.shape[0]
    for c in range(rows.shape[1] // LANES):
        out_ref[s * modes : (s + 1) * modes, c, :] = rows[:, c * LANES : (c + 1) * LANES]


def grown_rows(g_ref, s, modes):
    return jnp.concatenate([g_ref[s * modes : (s + 1) * modes, c, :] for c in range(g_ref.shape[1])], axis=1)


def inverse_factor(rows):
    modes = rows.shape[0]
    index = lax.broadcasted_iota(jnp.int32, (modes, 1), 0)
    taken = lax.broadcasted_iota(jnp.int32, (modes, LANES), 0) == lax.broadcasted_iota(jnp.int32, (modes, LANES), 1)
    taken = taken.astype(jnp.float32)
    for j in range(modes - 1):
        pivot = rows[j : j + 1]
        prods = jnp.sum(rows * pivot, axis=1, keepdims=True)
        ratio = jnp.where(index > j, prods / prods[j : j + 1], 0.0)
        rows = rows - ratio * pivot
        taken = taken - ratio * taken[j : j + 1]
    norms = jnp.sum(rows * rows, axis=1, keepdims=True)
    inverse = lax.rsqrt(norms)
    inverse = inverse * (1.5 - 0.5 * norms * inverse * inverse)
    return taken * inverse


def mixed(factor, rows):
    total = factor[:, 0:1] * rows[0:1]
    for j in range(1, rows.shape[0]):
        total = total + factor[:, j : j + 1] * rows[j : j + 1]
    return total


def first_kernel(scale, x_ref, start_ref, out_ref):
    for s in range(x_ref.shape[1]):
        x_parts = parts_of(cube_of(x_ref, s), 3)
        weights = products(start_ref[s], x_parts, INNER) * scale
        store_rows(out_ref, products(weights, x_parts, ROWS), s)


def turned_rows(rows, table_ref):
    turned = [
        products(half, [table_ref[p, parity] for p in range(3)], ROWS) for parity, half in enumerate(folded(rows, 1))
    ]
    half = turned[0].shape[1] // 2
    return jnp.concatenate([turned[q % 2][:, q // 2 * half : (q // 2 + 1) * half] for q in range(GROUPS)], axis=1)


def transform_kernel(x_ref, table_ref, out_ref):
    for s in range(x_ref.shape[1]):
        halves = []
        for parity, x in enumerate(folded(cube_of(x_ref, s), 0)):
            halves.append(products_of_parts([table_ref[p, parity] for p in range(3)], parts_of(x, 3), INNER))
        half = halves[0].shape[0] // 2
        turned = [halves[q % 2][q // 2 * half : (q // 2 + 1) * half] for q in range(GROUPS)]
        store_turned(out_ref, jnp.concatenate(turned, axis=0), s)


def second_kernel(scale, modes, x_ref, g_ref, table_ref, out_ref):
    species = range(x_ref.shape[1])
    grown = [grown_rows(g_ref, s, modes) for s in species]
    x_parts = [parts_of(turned_cube(x_ref, s), 3) for s in species]
    turned = turned_rows(jnp.concatenate(grown, axis=0), table_ref)
    raised = [products(turned[s * modes : (s + 1) * modes], x_parts[s], INNER) for s in species]
    factors = [inverse_factor(rows) for rows in grown]
    for s in species:
        store_rows(out_ref, products(mixed(factors[s], raised[s]) * scale, x_parts[s], ROWS), s)


def last_kernel(modes, x_ref, g_ref, out_ref, held):
    owners, _, tiles, rows, _ = out_ref.shape
    count = rows // GROUPS
    species = range(x_ref.shape[1])
    grown = [grown_rows(g_ref, s, modes) for s in species]
    cubes = [turned_cube(x_ref, s) for s in species]
    raised = [products(rows, parts_of(x, 3), INNER) for x, rows in zip(cubes, grown)]
    factors = [inverse_factor(rows) for rows in grown]
    for s in species:
        fix = expand(mixed(factors[s], grown[s]), mixed(factors[s], raised[s]))
        cleaned = cubes[s] - fix
        scaled = cleaned * np.float32(np.sqrt(0.5))
        for q in range(GROUPS):
            rows = pl.ds(q // 2 * count * 2 + q % 2, count, stride=2)
            for c in range(tiles):
                part = scaled[q * owners * count : (q + 1) * owners * count, c * LANES : (c + 1) * LANES]
                held[s, :, c, rows, :] = part.reshape(owners, count, LANES)
        out_ref[:, s] = held[s, :, :, : count * GROUPS]
        for c in range(tiles):
            out_ref[0, s, c, 0:1, :] = cleaned[0:1, c * LANES : (c + 1) * LANES]
            out_ref[0, s, c, 2 * count : 2 * count + 1, :] = jnp.zeros((1, LANES), jnp.float32)


def join_kernel(src, dst, held, sems):
    halves, species, waves, _ = dst.shape
    copies = []
    for h in range(halves):
        for s in range(species):
            for j in range(src.shape[0]):
                for c in range(src.shape[2]):
                    at = (j * src.shape[2] + c) * LANES
                    held[h, s, :, at : at + LANES] = src[j, s, c, h * waves : (h + 1) * waves]
            copy = pltpu.make_async_copy(held.at[h, s], dst.at[h, s], sems.at[h, s])
            copy.start()
            copies.append(copy)
    for copy in copies:
        copy.wait()


def tables(owners, waves, width):
    k = np.arange(waves)[:, None]
    f = np.arange(width // 2)[None, :]
    phase = 2.0 * np.pi * (k * f % width) / width
    both = np.stack([np.cos(phase), -np.sin(phase)]) * np.sqrt(2.0 / width)
    both[0, 0] = 1.0 / np.sqrt(width)
    both[1, 0] = (1.0 - 2.0 * (f[0] % 2)) / np.sqrt(width)
    left = both.reshape(2, owners, waves // owners // 2, 2, width // 2).transpose(3, 0, 1, 2, 4).reshape(2, waves, width // 2)
    parts = []
    for _ in range(3):
        part = left.astype(jnp.bfloat16)
        parts.append(part)
        left = left - part.astype(np.float64)
    return np.stack(parts)


def body(cubes, start_block):
    owners = lax.axis_size("chan")
    species, chans, pixels = cubes.shape
    width = chans * owners
    modes = start_block.shape[2]
    waves = width // 2
    step = pixels // owners
    scale = 1.0 / (pixels * lax.axis_size("pix"))
    share = shape(species * modes, width // LANES, LANES)
    split_shape = shape(owners, species, chans, step)
    table = jnp.asarray(tables(owners, waves, width))
    work = 2 * species * width * step
    grant = params(24)

    split = pl.pallas_call(
        split_kernel,
        out_shape=split_shape, in_specs=[VMEM], out_specs=VMEM, compiler_params=params(4),
    )(cubes)
    x = swap(split, "chan")
    part = pl.pallas_call(
        lambda *refs: first_kernel(scale, *refs),
        out_shape=share, in_specs=[VMEM, VMEM], out_specs=VMEM, compiler_params=grant,
        cost_estimate=cost(12 * modes * work, work),
    )(x, jnp.swapaxes(start_block, 1, 2))

    row = jnp.sum(swap(part, "chan"), axis=0)
    row, given = after(row, x)
    x = pl.pallas_call(
        transform_kernel,
        out_shape=split_shape, in_specs=[VMEM, VMEM], out_specs=VMEM, input_output_aliases={0: 0},
        compiler_params=grant, cost_estimate=cost(6 * waves * work, 6 * work),
    )(given, table)
    row = jnp.sum(to_all(row, "pix"), axis=0)
    row, x = after(row, x)
    grown = to_all(row, "chan")
    part = pl.pallas_call(
        lambda *refs: second_kernel(scale, modes, *refs),
        out_shape=share, in_specs=[VMEM, VMEM, VMEM], out_specs=VMEM, compiler_params=grant,
    )(x, grown, table)
    row = jnp.sum(swap(part, "chan"), axis=0)
    row = jnp.sum(to_all(row, "pix"), axis=0)
    grown = to_all(row, "chan")
    blocks = pl.pallas_call(
        lambda *refs: last_kernel(modes, *refs),
        out_shape=shape(owners, species, step // LANES, chans, LANES), in_specs=[VMEM, VMEM], out_specs=VMEM, compiler_params=grant,
        scratch_shapes=[pltpu.VMEM((species, owners, step // LANES, chans + 8, LANES), jnp.float32)],
    )(x, grown)
    return pl.pallas_call(
        join_kernel,
        out_shape=shape(2, species, waves // owners, pixels), in_specs=[VMEM], out_specs=HBM, compiler_params=params(8),
        scratch_shapes=[pltpu.VMEM((2, species, waves // owners, pixels), jnp.float32), DMA((2, species))],
    )(swap(blocks, "chan"))


def solution(mesh):
    placed = (P(None, "chan", "pix"), P())
    return jax.shard_map(
        body, mesh=mesh, in_specs=placed, out_specs=P(None, None, "chan", "pix"), check_vma=False
    )
```

```python
import jax
import jax.numpy as jnp
import numpy as np
from jax import lax
from jax.experimental import pallas as pl
from jax.experimental.pallas import tpu as pltpu
from jax.sharding import PartitionSpec as P

ITERS = 2
LANES = 128
GROUPS = 4
INNER, ROWS, OUTER = ((1,), (0,)), ((1,), (1,)), ((0,), (0,))
VMEM = pl.BlockSpec(memory_space=pltpu.VMEM)
HBM = pl.BlockSpec(memory_space=pltpu.HBM)
DMA = pltpu.SemaphoreType.DMA


def params(mib):
    return pltpu.CompilerParams(vmem_limit_bytes=mib * 1024 * 1024)


def swap(value, axis):
    return lax.all_to_all(value, axis, split_axis=0, concat_axis=0, tiled=True)


def to_all(value, axis):
    count = lax.axis_size(axis)
    return swap(jnp.broadcast_to(value[None], (count,) + value.shape), axis)


def after(value, others):
    return lax.optimization_barrier((value, others))


def cost(flops, moved):
    return pl.CostEstimate(flops=flops, bytes_accessed=moved, transcendentals=0)


def shape(*dims):
    return jax.ShapeDtypeStruct(dims, jnp.float32)


def dot(a, b, dims):
    return lax.dot_general(a, b, (dims, ((), ())), preferred_element_type=jnp.float32)


def cube_of(x_ref, s):
    parts, _, chans, pixels = x_ref.shape
    return x_ref[:, s].reshape(parts * chans, pixels)


def turned_cube(x_ref, s):
    owners, _, rows, pixels = x_ref.shape
    step = rows // GROUPS
    groups = [x_ref[:, s, q * step : (q + 1) * step].reshape(owners * step, pixels) for q in range(GROUPS)]
    return jnp.concatenate(groups, axis=0)


def store_turned(out_ref, value, s):
    owners, _, rows, pixels = out_ref.shape
    step = rows // GROUPS
    for q in range(GROUPS):
        part = value[q * owners * step : (q + 1) * owners * step]
        out_ref[:, s, q * step : (q + 1) * step] = part.reshape(owners, step, pixels)


def folded(value, axis):
    half = value.shape[axis] // 2
    first, second = lax.slice_in_dim(value, 0, half, axis=axis), lax.slice_in_dim(value, half, 2 * half, axis=axis)
    return first + second, first - second


def parts_of(value, count):
    parts = []
    for _ in range(count):
        part = value.astype(jnp.bfloat16)
        parts.append(part)
        value = value - part.astype(jnp.float32)
    return parts


def split_kernel(src, dst):
    step = dst.shape[3]
    for j in range(dst.shape[0]):
        dst[j] = src[:, :, j * step : (j + 1) * step]


def products_of_parts(left, right, dims):
    count = left[0].shape[0]
    stacked = jnp.concatenate(left, axis=0)
    a = dot(stacked, right[0], dims)
    b = dot(stacked[: 2 * count], right[1], dims)
    c = dot(stacked[:count], right[2], dims)
    return a[:count] + ((a[count : 2 * count] + b[:count]) + ((a[2 * count :] + b[count:]) + c))


def products(rows, right, dims):
    count = rows.shape[0]
    stacked = jnp.concatenate([part.astype(jnp.float32) for part in parts_of(rows, 3)], axis=0).astype(jnp.bfloat16)
    a = dot(stacked, right[0], dims)
    b = dot(stacked[: 2 * count], right[1], dims)
    c = dot(stacked[:count], right[2], dims)
    return a[:count] + ((a[count : 2 * count] + b[:count]) + ((a[2 * count :] + b[count:]) + c))


def expand(rows, weights):
    left = [part.astype(jnp.float32) for part in parts_of(rows, 3)]
    right = [part.astype(jnp.float32) for part in parts_of(weights, 3)]
    pairs = [(0, 0), (0, 1), (1, 0), (0, 2), (1, 1), (2, 0)]
    left = jnp.concatenate([left[a] for a, _ in pairs], axis=0).astype(jnp.bfloat16)
    right = jnp.concatenate([right[b] for _, b in pairs], axis=0).astype(jnp.bfloat16)
    return dot(left, right, OUTER)


def store_rows(out_ref, rows, s):
    modes = rows.shape[0]
    for c in range(rows.shape[1] // LANES):
        out_ref[s * modes : (s + 1) * modes, c, :] = rows[:, c * LANES : (c + 1) * LANES]


def grown_rows(g_ref, s, modes):
    return jnp.concatenate([g_ref[s * modes : (s + 1) * modes, c, :] for c in range(g_ref.shape[1])], axis=1)


def orthonormal(rows):
    modes = rows.shape[0]
    index = lax.broadcasted_iota(jnp.int32, (modes, 1), 0)
    for j in range(modes - 1):
        pivot = rows[j : j + 1]
        prods = jnp.sum(rows * pivot, axis=1, keepdims=True)
        ratio = jnp.where(index > j, prods / prods[j : j + 1], 0.0)
        rows = rows - ratio * pivot
    norms = jnp.sum(rows * rows, axis=1, keepdims=True)
    inverse = lax.rsqrt(norms)
    inverse = inverse * (1.5 - 0.5 * norms * inverse * inverse)
    return rows * inverse


def first_kernel(scale, x_ref, start_ref, table_ref, out_ref):
    grown = []
    for s in range(x_ref.shape[1]):
        x_parts = parts_of(cube_of(x_ref, s), 3)
        weights = products(start_ref[s], x_parts, INNER) * scale
        grown.append(products(weights, x_parts, ROWS))
    turned = [
        products(rows, [table_ref[p, parity] for p in range(3)], ROWS)
        for parity, rows in enumerate(folded(jnp.concatenate(grown, axis=0), 1))
    ]
    half = turned[0].shape[1] // 2
    turned = [turned[q % 2][:, q // 2 * half : (q // 2 + 1) * half] for q in range(GROUPS)]
    store_rows(out_ref, jnp.concatenate(turned, axis=1), 0)


def transform_kernel(x_ref, table_ref, out_ref):
    for s in range(x_ref.shape[1]):
        halves = []
        for parity, x in enumerate(folded(cube_of(x_ref, s), 0)):
            halves.append(products_of_parts([table_ref[p, parity] for p in range(3)], parts_of(x, 3), INNER))
        half = halves[0].shape[0] // 2
        turned = [halves[q % 2][q // 2 * half : (q // 2 + 1) * half] for q in range(GROUPS)]
        store_turned(out_ref, jnp.concatenate(turned, axis=0), s)


def next_kernel(scale, modes, x_ref, g_ref, out_ref):
    species = range(x_ref.shape[1])
    bases = [orthonormal(grown_rows(g_ref, s, modes)) for s in species]
    x_parts = [parts_of(turned_cube(x_ref, s), 3) for s in species]
    weights = [products(basis, parts, INNER) * scale for basis, parts in zip(bases, x_parts)]
    for s in species:
        store_rows(out_ref, products(weights[s], x_parts[s], ROWS), s)


def last_kernel(modes, x_ref, g_ref, out_ref, held):
    owners, _, tiles, rows, _ = out_ref.shape
    count = rows // GROUPS
    species = range(x_ref.shape[1])
    bases = [orthonormal(grown_rows(g_ref, s, modes)) for s in species]
    cubes = [turned_cube(x_ref, s) for s in species]
    weights = [products(basis, parts_of(x, 3), INNER) for basis, x in zip(bases, cubes)]
    for s in species:
        fix = expand(bases[s], weights[s])
        cleaned = cubes[s] - fix
        scaled = cleaned * np.float32(np.sqrt(0.5))
        for q in range(GROUPS):
            rows = pl.ds(q // 2 * count * 2 + q % 2, count, stride=2)
            for c in range(tiles):
                part = scaled[q * owners * count : (q + 1) * owners * count, c * LANES : (c + 1) * LANES]
                held[s, :, c, rows, :] = part.reshape(owners, count, LANES)
        out_ref[:, s] = held[s, :, :, : count * GROUPS]
        for c in range(tiles):
            out_ref[0, s, c, 0:1, :] = cleaned[0:1, c * LANES : (c + 1) * LANES]
            out_ref[0, s, c, 2 * count : 2 * count + 1, :] = jnp.zeros((1, LANES), jnp.float32)


def join_kernel(src, dst, held, sems):
    halves, species, waves, _ = dst.shape
    copies = []
    for h in range(halves):
        for s in range(species):
            for j in range(src.shape[0]):
                for c in range(src.shape[2]):
                    at = (j * src.shape[2] + c) * LANES
                    held[h, s, :, at : at + LANES] = src[j, s, c, h * waves : (h + 1) * waves]
            copy = pltpu.make_async_copy(held.at[h, s], dst.at[h, s], sems.at[h, s])
            copy.start()
            copies.append(copy)
    for copy in copies:
        copy.wait()


def tables(owners, waves, width):
    k = np.arange(waves)[:, None]
    f = np.arange(width // 2)[None, :]
    phase = 2.0 * np.pi * (k * f % width) / width
    both = np.stack([np.cos(phase), -np.sin(phase)]) * np.sqrt(2.0 / width)
    both[0, 0] = 1.0 / np.sqrt(width)
    both[1, 0] = (1.0 - 2.0 * (f[0] % 2)) / np.sqrt(width)
    left = both.reshape(2, owners, waves // owners // 2, 2, width // 2).transpose(3, 0, 1, 2, 4).reshape(2, waves, width // 2)
    parts = []
    for _ in range(3):
        part = left.astype(jnp.bfloat16)
        parts.append(part)
        left = left - part.astype(np.float64)
    return np.stack(parts)


def body(cubes, start_block):
    owners = lax.axis_size("chan")
    species, chans, pixels = cubes.shape
    width = chans * owners
    modes = start_block.shape[2]
    waves = width // 2
    step = pixels // owners
    scale = 1.0 / (pixels * lax.axis_size("pix"))
    share = shape(species * modes, width // LANES, LANES)
    split_shape = shape(owners, species, chans, step)
    table = jnp.asarray(tables(owners, waves, width))
    work = 2 * species * width * step
    grant = params(24)

    split = pl.pallas_call(
        split_kernel,
        out_shape=split_shape, in_specs=[VMEM], out_specs=VMEM, compiler_params=params(4),
    )(cubes)
    x = swap(split, "chan")
    part = pl.pallas_call(
        lambda *refs: first_kernel(scale, *refs),
        out_shape=share, in_specs=[VMEM, VMEM, VMEM], out_specs=VMEM, compiler_params=grant,
        cost_estimate=cost(12 * modes * work, work),
    )(x, jnp.swapaxes(start_block, 1, 2), table)

    row = jnp.sum(swap(part, "chan"), axis=0)
    row, given = after(row, x)
    x = pl.pallas_call(
        transform_kernel,
        out_shape=split_shape, in_specs=[VMEM, VMEM], out_specs=VMEM, input_output_aliases={0: 0},
        compiler_params=grant, cost_estimate=cost(6 * waves * work, 6 * work),
    )(given, table)
    row = jnp.sum(to_all(row, "pix"), axis=0)
    row, x = after(row, x)
    grown = to_all(row, "chan")
    for _ in range(ITERS - 1):
        part = pl.pallas_call(
            lambda *refs: next_kernel(scale, modes, *refs),
            out_shape=share, in_specs=[VMEM, VMEM], out_specs=VMEM, compiler_params=grant,
        )(x, grown)
        row = jnp.sum(swap(part, "chan"), axis=0)
        row = jnp.sum(to_all(row, "pix"), axis=0)
        grown = to_all(row, "chan")
    blocks = pl.pallas_call(
        lambda *refs: last_kernel(modes, *refs),
        out_shape=shape(owners, species, step // LANES, chans, LANES), in_specs=[VMEM, VMEM], out_specs=VMEM, compiler_params=grant,
        scratch_shapes=[pltpu.VMEM((species, owners, step // LANES, chans + 8, LANES), jnp.float32)],
    )(x, grown)
    return pl.pallas_call(
        join_kernel,
        out_shape=shape(2, species, waves // owners, pixels), in_specs=[VMEM], out_specs=HBM, compiler_params=params(8),
        scratch_shapes=[pltpu.VMEM((2, species, waves // owners, pixels), jnp.float32), DMA((2, species))],
    )(swap(blocks, "chan"))


def solution(mesh):
    placed = (P(None, "chan", "pix"), P())
    return jax.shard_map(
        body, mesh=mesh, in_specs=placed, out_specs=P(None, None, "chan", "pix"), check_vma=False
    )
```

```python
import jax
import jax.numpy as jnp
import numpy as np
from jax import lax
from jax.experimental import pallas as pl
from jax.experimental.pallas import tpu as pltpu
from jax.sharding import PartitionSpec as P

LANES = 128
GROUPS = 4
INNER, ROWS, OUTER = ((1,), (0,)), ((1,), (1,)), ((0,), (0,))
VMEM = pl.BlockSpec(memory_space=pltpu.VMEM)
HBM = pl.BlockSpec(memory_space=pltpu.HBM)
DMA = pltpu.SemaphoreType.DMA


def params(mib):
    return pltpu.CompilerParams(vmem_limit_bytes=mib * 1024 * 1024)


def swap(value, axis):
    return lax.all_to_all(value, axis, split_axis=0, concat_axis=0, tiled=True)


def to_all(value, axis):
    count = lax.axis_size(axis)
    return swap(jnp.broadcast_to(value[None], (count,) + value.shape), axis)


def after(value, others):
    return lax.optimization_barrier((value, others))


def cost(flops, moved):
    return pl.CostEstimate(flops=flops, bytes_accessed=moved, transcendentals=0)


def shape(*dims):
    return jax.ShapeDtypeStruct(dims, jnp.float32)


def dot(a, b, dims):
    return lax.dot_general(a, b, (dims, ((), ())), preferred_element_type=jnp.float32)


def cube_of(x_ref, s):
    parts, _, chans, pixels = x_ref.shape
    return x_ref[:, s].reshape(parts * chans, pixels)


def turned_cube(x_ref, s):
    owners, _, rows, pixels = x_ref.shape
    step = rows // GROUPS
    groups = [x_ref[:, s, q * step : (q + 1) * step].reshape(owners * step, pixels) for q in range(GROUPS)]
    return jnp.concatenate(groups, axis=0)


def store_turned(out_ref, value, s):
    owners, _, rows, pixels = out_ref.shape
    step = rows // GROUPS
    for q in range(GROUPS):
        part = value[q * owners * step : (q + 1) * owners * step]
        out_ref[:, s, q * step : (q + 1) * step] = part.reshape(owners, step, pixels)


def folded(value, axis):
    half = value.shape[axis] // 2
    first, second = lax.slice_in_dim(value, 0, half, axis=axis), lax.slice_in_dim(value, half, 2 * half, axis=axis)
    return first + second, first - second


def parts_of(value, count):
    parts = []
    for _ in range(count):
        part = value.astype(jnp.bfloat16)
        parts.append(part)
        value = value - part.astype(jnp.float32)
    return parts


def split_kernel(src, dst):
    step = dst.shape[3]
    for j in range(dst.shape[0]):
        dst[j] = src[:, :, j * step : (j + 1) * step]


def products_of_parts(left, right, dims):
    count = left[0].shape[0]
    stacked = jnp.concatenate(left, axis=0)
    a = dot(stacked, right[0], dims)
    b = dot(stacked[: 2 * count], right[1], dims)
    c = dot(stacked[:count], right[2], dims)
    return a[:count] + ((a[count : 2 * count] + b[:count]) + ((a[2 * count :] + b[count:]) + c))


def products(rows, right, dims):
    count = rows.shape[0]
    stacked = jnp.concatenate([part.astype(jnp.float32) for part in parts_of(rows, 3)], axis=0).astype(jnp.bfloat16)
    a = dot(stacked, right[0], dims)
    b = dot(stacked[: 2 * count], right[1], dims)
    c = dot(stacked[:count], right[2], dims)
    return a[:count] + ((a[count : 2 * count] + b[:count]) + ((a[2 * count :] + b[count:]) + c))


def expand(rows, weights):
    left = [part.astype(jnp.float32) for part in parts_of(rows, 3)]
    right = [part.astype(jnp.float32) for part in parts_of(weights, 3)]
    pairs = [(0, 0), (0, 1), (1, 0), (0, 2), (1, 1), (2, 0)]
    left = jnp.concatenate([left[a] for a, _ in pairs], axis=0).astype(jnp.bfloat16)
    right = jnp.concatenate([right[b] for _, b in pairs], axis=0).astype(jnp.bfloat16)
    return dot(left, right, OUTER)


def store_rows(out_ref, rows, s):
    modes = rows.shape[0]
    for c in range(rows.shape[1] // LANES):
        out_ref[s * modes : (s + 1) * modes, c, :] = rows[:, c * LANES : (c + 1) * LANES]


def grown_rows(g_ref, s, modes):
    return jnp.concatenate([g_ref[s * modes : (s + 1) * modes, c, :] for c in range(g_ref.shape[1])], axis=1)


def orthonormal(rows):
    modes = rows.shape[0]
    index = lax.broadcasted_iota(jnp.int32, (modes, 1), 0)
    for j in range(modes - 1):
        pivot = rows[j : j + 1]
        prods = jnp.sum(rows * pivot, axis=1, keepdims=True)
        ratio = jnp.where(index > j, prods / prods[j : j + 1], 0.0)
        rows = rows - ratio * pivot
    norms = jnp.sum(rows * rows, axis=1, keepdims=True)
    inverse = lax.rsqrt(norms)
    inverse = inverse * (1.5 - 0.5 * norms * inverse * inverse)
    return rows * inverse


def inverse_factor(rows):
    modes = rows.shape[0]
    index = lax.broadcasted_iota(jnp.int32, (modes, 1), 0)
    taken = lax.broadcasted_iota(jnp.int32, (modes, LANES), 0) == lax.broadcasted_iota(jnp.int32, (modes, LANES), 1)
    taken = taken.astype(jnp.float32)
    for j in range(modes - 1):
        pivot = rows[j : j + 1]
        prods = jnp.sum(rows * pivot, axis=1, keepdims=True)
        ratio = jnp.where(index > j, prods / prods[j : j + 1], 0.0)
        rows = rows - ratio * pivot
        taken = taken - ratio * taken[j : j + 1]
    norms = jnp.sum(rows * rows, axis=1, keepdims=True)
    inverse = lax.rsqrt(norms)
    inverse = inverse * (1.5 - 0.5 * norms * inverse * inverse)
    return taken * inverse


def mixed(factor, rows):
    total = factor[:, 0:1] * rows[0:1]
    for j in range(1, rows.shape[0]):
        total = total + factor[:, j : j + 1] * rows[j : j + 1]
    return total


def first_kernel(scale, x_ref, start_ref, out_ref):
    for s in range(x_ref.shape[1]):
        x_parts = parts_of(cube_of(x_ref, s), 3)
        weights = products(start_ref[s], x_parts, INNER) * scale
        store_rows(out_ref, products(weights, x_parts, ROWS), s)


def turned_rows(rows, table_ref):
    turned = [
        products(half, [table_ref[p, parity] for p in range(3)], ROWS) for parity, half in enumerate(folded(rows, 1))
    ]
    half = turned[0].shape[1] // 2
    return jnp.concatenate([turned[q % 2][:, q // 2 * half : (q // 2 + 1) * half] for q in range(GROUPS)], axis=1)


def transform_kernel(x_ref, table_ref, out_ref):
    for s in range(x_ref.shape[1]):
        halves = []
        for parity, x in enumerate(folded(cube_of(x_ref, s), 0)):
            halves.append(products_of_parts([table_ref[p, parity] for p in range(3)], parts_of(x, 3), INNER))
        half = halves[0].shape[0] // 2
        turned = [halves[q % 2][q // 2 * half : (q // 2 + 1) * half] for q in range(GROUPS)]
        store_turned(out_ref, jnp.concatenate(turned, axis=0), s)


def second_kernel(scale, modes, x_ref, g_ref, table_ref, out_ref):
    species = range(x_ref.shape[1])
    grown = [grown_rows(g_ref, s, modes) for s in species]
    turned = turned_rows(jnp.concatenate(grown, axis=0), table_ref)
    x_parts = [parts_of(turned_cube(x_ref, s), 3) for s in species]
    bases = [mixed(inverse_factor(grown[s]), turned[s * modes : (s + 1) * modes]) for s in species]
    weights = [products(basis, parts, INNER) * scale for basis, parts in zip(bases, x_parts)]
    for s in species:
        store_rows(out_ref, products(weights[s], x_parts[s], ROWS), s)


def last_kernel(modes, x_ref, g_ref, out_ref, held):
    owners, _, tiles, rows, _ = out_ref.shape
    count = rows // GROUPS
    species = range(x_ref.shape[1])
    bases = [orthonormal(grown_rows(g_ref, s, modes)) for s in species]
    cubes = [turned_cube(x_ref, s) for s in species]
    weights = [products(basis, parts_of(x, 3), INNER) for basis, x in zip(bases, cubes)]
    for s in species:
        fix = expand(bases[s], weights[s])
        cleaned = cubes[s] - fix
        scaled = cleaned * np.float32(np.sqrt(0.5))
        for q in range(GROUPS):
            rows = pl.ds(q // 2 * count * 2 + q % 2, count, stride=2)
            for c in range(tiles):
                part = scaled[q * owners * count : (q + 1) * owners * count, c * LANES : (c + 1) * LANES]
                held[s, :, c, rows, :] = part.reshape(owners, count, LANES)
        out_ref[:, s] = held[s, :, :, : count * GROUPS]
        for c in range(tiles):
            out_ref[0, s, c, 0:1, :] = cleaned[0:1, c * LANES : (c + 1) * LANES]
            out_ref[0, s, c, 2 * count : 2 * count + 1, :] = jnp.zeros((1, LANES), jnp.float32)


def join_kernel(src, dst, held, sems):
    halves, species, waves, _ = dst.shape
    copies = []
    for h in range(halves):
        for s in range(species):
            for j in range(src.shape[0]):
                for c in range(src.shape[2]):
                    at = (j * src.shape[2] + c) * LANES
                    held[h, s, :, at : at + LANES] = src[j, s, c, h * waves : (h + 1) * waves]
            copy = pltpu.make_async_copy(held.at[h, s], dst.at[h, s], sems.at[h, s])
            copy.start()
            copies.append(copy)
    for copy in copies:
        copy.wait()


def tables(owners, waves, width):
    k = np.arange(waves)[:, None]
    f = np.arange(width // 2)[None, :]
    phase = 2.0 * np.pi * (k * f % width) / width
    both = np.stack([np.cos(phase), -np.sin(phase)]) * np.sqrt(2.0 / width)
    both[0, 0] = 1.0 / np.sqrt(width)
    both[1, 0] = (1.0 - 2.0 * (f[0] % 2)) / np.sqrt(width)
    left = both.reshape(2, owners, waves // owners // 2, 2, width // 2).transpose(3, 0, 1, 2, 4).reshape(2, waves, width // 2)
    parts = []
    for _ in range(3):
        part = left.astype(jnp.bfloat16)
        parts.append(part)
        left = left - part.astype(np.float64)
    return np.stack(parts)


def body(cubes, start_block):
    owners = lax.axis_size("chan")
    species, chans, pixels = cubes.shape
    width = chans * owners
    modes = start_block.shape[2]
    waves = width // 2
    step = pixels // owners
    scale = 1.0 / (pixels * lax.axis_size("pix"))
    share = shape(species * modes, width // LANES, LANES)
    split_shape = shape(owners, species, chans, step)
    table = jnp.asarray(tables(owners, waves, width))
    work = 2 * species * width * step
    grant = params(24)

    split = pl.pallas_call(
        split_kernel,
        out_shape=split_shape, in_specs=[VMEM], out_specs=VMEM, compiler_params=params(4),
    )(cubes)
    x = swap(split, "chan")
    part = pl.pallas_call(
        lambda *refs: first_kernel(scale, *refs),
        out_shape=share, in_specs=[VMEM, VMEM], out_specs=VMEM, compiler_params=grant,
        cost_estimate=cost(12 * modes * work, work),
    )(x, jnp.swapaxes(start_block, 1, 2))

    row = jnp.sum(swap(part, "chan"), axis=0)
    row, given = after(row, x)
    x = pl.pallas_call(
        transform_kernel,
        out_shape=split_shape, in_specs=[VMEM, VMEM], out_specs=VMEM, input_output_aliases={0: 0},
        compiler_params=grant, cost_estimate=cost(6 * waves * work, 6 * work),
    )(given, table)
    row = jnp.sum(to_all(row, "pix"), axis=0)
    row, x = after(row, x)
    grown = to_all(row, "chan")
    part = pl.pallas_call(
        lambda *refs: second_kernel(scale, modes, *refs),
        out_shape=share, in_specs=[VMEM, VMEM, VMEM], out_specs=VMEM, compiler_params=grant,
    )(x, grown, table)
    row = jnp.sum(swap(part, "chan"), axis=0)
    row = jnp.sum(to_all(row, "pix"), axis=0)
    grown = to_all(row, "chan")
    blocks = pl.pallas_call(
        lambda *refs: last_kernel(modes, *refs),
        out_shape=shape(owners, species, step // LANES, chans, LANES), in_specs=[VMEM, VMEM], out_specs=VMEM, compiler_params=grant,
        scratch_shapes=[pltpu.VMEM((species, owners, step // LANES, chans + 8, LANES), jnp.float32)],
    )(x, grown)
    return pl.pallas_call(
        join_kernel,
        out_shape=shape(2, species, waves // owners, pixels), in_specs=[VMEM], out_specs=HBM, compiler_params=params(8),
        scratch_shapes=[pltpu.VMEM((2, species, waves // owners, pixels), jnp.float32), DMA((2, species))],
    )(swap(blocks, "chan"))


def solution(mesh):
    placed = (P(None, "chan", "pix"), P())
    return jax.shard_map(
        body, mesh=mesh, in_specs=placed, out_specs=P(None, None, "chan", "pix"), check_vma=False
    )
```

```python
import jax
import jax.numpy as jnp
import numpy as np
from jax import lax
from jax.experimental import pallas as pl
from jax.experimental.pallas import tpu as pltpu
from jax.sharding import PartitionSpec as P

LANES = 128
GROUPS = 4
INNER, ROWS, OUTER = ((1,), (0,)), ((1,), (1,)), ((0,), (0,))
VMEM = pl.BlockSpec(memory_space=pltpu.VMEM)
HBM = pl.BlockSpec(memory_space=pltpu.HBM)
DMA = pltpu.SemaphoreType.DMA


def params(mib):
    return pltpu.CompilerParams(vmem_limit_bytes=mib * 1024 * 1024)


def swap(value, axis):
    return lax.all_to_all(value, axis, split_axis=0, concat_axis=0, tiled=True)


def to_all(value, axis):
    count = lax.axis_size(axis)
    return swap(jnp.broadcast_to(value[None], (count,) + value.shape), axis)


def after(value, others):
    return lax.optimization_barrier((value, others))


def cost(flops, moved):
    return pl.CostEstimate(flops=flops, bytes_accessed=moved, transcendentals=0)


def shape(*dims):
    return jax.ShapeDtypeStruct(dims, jnp.float32)


def dot(a, b, dims):
    return lax.dot_general(a, b, (dims, ((), ())), preferred_element_type=jnp.float32)


def cube_of(x_ref, s):
    parts, _, chans, pixels = x_ref.shape
    return x_ref[:, s].reshape(parts * chans, pixels)


def turned_cube(x_ref, s):
    owners, _, rows, pixels = x_ref.shape
    step = rows // GROUPS
    groups = [x_ref[:, s, q * step : (q + 1) * step].reshape(owners * step, pixels) for q in range(GROUPS)]
    return jnp.concatenate(groups, axis=0)


def store_turned(out_ref, value, s):
    owners, _, rows, pixels = out_ref.shape
    step = rows // GROUPS
    for q in range(GROUPS):
        part = value[q * owners * step : (q + 1) * owners * step]
        out_ref[:, s, q * step : (q + 1) * step] = part.reshape(owners, step, pixels)


def folded(value, axis):
    half = value.shape[axis] // 2
    first, second = lax.slice_in_dim(value, 0, half, axis=axis), lax.slice_in_dim(value, half, 2 * half, axis=axis)
    return first + second, first - second


def parts_of(value, count):
    parts = []
    for _ in range(count):
        part = value.astype(jnp.bfloat16)
        parts.append(part)
        value = value - part.astype(jnp.float32)
    return parts


def split_kernel(src, dst):
    step = dst.shape[3]
    for j in range(dst.shape[0]):
        dst[j] = src[:, :, j * step : (j + 1) * step]


def products_of_parts(left, right, dims):
    count = left[0].shape[0]
    stacked = jnp.concatenate(left, axis=0)
    a = dot(stacked, right[0], dims)
    b = dot(stacked[: 2 * count], right[1], dims)
    c = dot(stacked[:count], right[2], dims)
    return a[:count] + ((a[count : 2 * count] + b[:count]) + ((a[2 * count :] + b[count:]) + c))


def products(rows, right, dims):
    count = rows.shape[0]
    stacked = jnp.concatenate([part.astype(jnp.float32) for part in parts_of(rows, 3)], axis=0).astype(jnp.bfloat16)
    a = dot(stacked, right[0], dims)
    b = dot(stacked[: 2 * count], right[1], dims)
    c = dot(stacked[:count], right[2], dims)
    return a[:count] + ((a[count : 2 * count] + b[:count]) + ((a[2 * count :] + b[count:]) + c))


def expand(rows, weights):
    left = [part.astype(jnp.float32) for part in parts_of(rows, 3)]
    right = [part.astype(jnp.float32) for part in parts_of(weights, 3)]
    pairs = [(0, 0), (0, 1), (1, 0), (0, 2), (1, 1), (2, 0)]
    left = jnp.concatenate([left[a] for a, _ in pairs], axis=0).astype(jnp.bfloat16)
    right = jnp.concatenate([right[b] for _, b in pairs], axis=0).astype(jnp.bfloat16)
    return dot(left, right, OUTER)


def store_rows(out_ref, rows, s):
    modes = rows.shape[0]
    for c in range(rows.shape[1] // LANES):
        out_ref[s * modes : (s + 1) * modes, c, :] = rows[:, c * LANES : (c + 1) * LANES]


def grown_rows(g_ref, s, modes):
    return jnp.concatenate([g_ref[s * modes : (s + 1) * modes, c, :] for c in range(g_ref.shape[1])], axis=1)


def orthonormal(rows):
    modes = rows.shape[0]
    index = lax.broadcasted_iota(jnp.int32, (modes, 1), 0)
    for j in range(modes - 1):
        pivot = rows[j : j + 1]
        prods = jnp.sum(rows * pivot, axis=1, keepdims=True)
        ratio = jnp.where(index > j, prods / prods[j : j + 1], 0.0)
        rows = rows - ratio * pivot
    norms = jnp.sum(rows * rows, axis=1, keepdims=True)
    inverse = lax.rsqrt(norms)
    inverse = inverse * (1.5 - 0.5 * norms * inverse * inverse)
    return rows * inverse


def inverse_factor(rows):
    modes = rows.shape[0]
    index = lax.broadcasted_iota(jnp.int32, (modes, 1), 0)
    taken = lax.broadcasted_iota(jnp.int32, (modes, LANES), 0) == lax.broadcasted_iota(jnp.int32, (modes, LANES), 1)
    taken = taken.astype(jnp.float32)
    for j in range(modes - 1):
        pivot = rows[j : j + 1]
        prods = jnp.sum(rows * pivot, axis=1, keepdims=True)
        ratio = jnp.where(index > j, prods / prods[j : j + 1], 0.0)
        rows = rows - ratio * pivot
        taken = taken - ratio * taken[j : j + 1]
    norms = jnp.sum(rows * rows, axis=1, keepdims=True)
    inverse = lax.rsqrt(norms)
    inverse = inverse * (1.5 - 0.5 * norms * inverse * inverse)
    return taken * inverse


def mixed(factor, rows):
    total = factor[:, 0:1] * rows[0:1]
    for j in range(1, rows.shape[0]):
        total = total + factor[:, j : j + 1] * rows[j : j + 1]
    return total


def first_kernel(scale, x_ref, start_ref, out_ref):
    for s in range(x_ref.shape[1]):
        x_parts = parts_of(cube_of(x_ref, s), 3)
        weights = products(start_ref[s], x_parts, INNER) * scale
        store_rows(out_ref, products(weights, x_parts, ROWS), s)


def turned_rows(rows, table_ref):
    turned = [
        products(half, [table_ref[p, parity] for p in range(3)], ROWS) for parity, half in enumerate(folded(rows, 1))
    ]
    half = turned[0].shape[1] // 2
    return jnp.concatenate([turned[q % 2][:, q // 2 * half : (q // 2 + 1) * half] for q in range(GROUPS)], axis=1)


def transform_kernel(x_ref, table_ref, out_ref):
    for s in range(x_ref.shape[1]):
        halves = []
        for parity, x in enumerate(folded(cube_of(x_ref, s), 0)):
            halves.append(products_of_parts([table_ref[p, parity] for p in range(3)], parts_of(x, 3), INNER))
        half = halves[0].shape[0] // 2
        turned = [halves[q % 2][q // 2 * half : (q // 2 + 1) * half] for q in range(GROUPS)]
        store_turned(out_ref, jnp.concatenate(turned, axis=0), s)


def second_kernel(scale, modes, x_ref, g_ref, table_ref, out_ref):
    species = range(x_ref.shape[1])
    grown = [grown_rows(g_ref, s, modes) for s in species]
    turned = turned_rows(jnp.concatenate(grown, axis=0), table_ref)
    x_parts = [parts_of(turned_cube(x_ref, s), 3) for s in species]
    bases = [mixed(inverse_factor(grown[s]), turned[s * modes : (s + 1) * modes]) for s in species]
    weights = [products(basis, parts, INNER) * scale for basis, parts in zip(bases, x_parts)]
    for s in species:
        store_rows(out_ref, products(weights[s], x_parts[s], ROWS), s)


def last_kernel(modes, x_ref, g_ref, out_ref, held):
    owners, _, tiles, rows, _ = out_ref.shape
    count = rows // GROUPS
    species = range(x_ref.shape[1])
    bases = [orthonormal(grown_rows(g_ref, s, modes)) for s in species]
    cubes = [turned_cube(x_ref, s) for s in species]
    weights = [products(basis, parts_of(x, 3), INNER) for basis, x in zip(bases, cubes)]
    for s in species:
        fix = expand(bases[s], weights[s])
        cleaned = cubes[s] - fix
        scaled = cleaned * np.float32(np.sqrt(0.5))
        for q in range(GROUPS):
            rows = pl.ds(q // 2 * count * 2 + q % 2, count, stride=2)
            for c in range(tiles):
                part = scaled[q * owners * count : (q + 1) * owners * count, c * LANES : (c + 1) * LANES]
                held[s, :, c, rows, :] = part.reshape(owners, count, LANES)
        out_ref[:, s] = held[s, :, :, : count * GROUPS]
        for c in range(tiles):
            out_ref[0, s, c, 0:1, :] = cleaned[0:1, c * LANES : (c + 1) * LANES]
            out_ref[0, s, c, 2 * count : 2 * count + 1, :] = jnp.zeros((1, LANES), jnp.float32)


def join_kernel(src, dst, held, sems):
    halves, species, waves, _ = dst.shape
    copies = []
    for h in range(halves):
        for s in range(species):
            for j in range(src.shape[0]):
                for c in range(src.shape[2]):
                    at = (j * src.shape[2] + c) * LANES
                    held[h, s, :, at : at + LANES] = src[j, s, c, h * waves : (h + 1) * waves]
            copy = pltpu.make_async_copy(held.at[h, s], dst.at[h, s], sems.at[h, s])
            copy.start()
            copies.append(copy)
    for copy in copies:
        copy.wait()


def tables(owners, waves, width):
    k = np.arange(waves)[:, None]
    f = np.arange(width // 2)[None, :]
    phase = 2.0 * np.pi * (k * f % width) / width
    both = np.stack([np.cos(phase), -np.sin(phase)]) * np.sqrt(2.0 / width)
    both[0, 0] = 1.0 / np.sqrt(width)
    both[1, 0] = (1.0 - 2.0 * (f[0] % 2)) / np.sqrt(width)
    left = both.reshape(2, owners, waves // owners // 2, 2, width // 2).transpose(3, 0, 1, 2, 4).reshape(2, waves, width // 2)
    parts = []
    for _ in range(3):
        part = left.astype(jnp.bfloat16)
        parts.append(part)
        left = left - part.astype(np.float64)
    return np.stack(parts)


def body(cubes, start_block):
    owners = lax.axis_size("chan")
    species, chans, pixels = cubes.shape
    width = chans * owners
    modes = start_block.shape[2]
    waves = width // 2
    step = pixels // owners
    scale = 1.0 / (pixels * lax.axis_size("pix"))
    share = shape(species * modes, width // LANES, LANES)
    split_shape = shape(owners, species, chans, step)
    table = jnp.asarray(tables(owners, waves, width))
    work = 2 * species * width * step
    grant = params(24)

    split = pl.pallas_call(
        split_kernel,
        out_shape=split_shape, in_specs=[VMEM], out_specs=VMEM, compiler_params=params(4),
    )(cubes)
    x = swap(split, "chan")
    part = pl.pallas_call(
        lambda *refs: first_kernel(scale, *refs),
        out_shape=share, in_specs=[VMEM, VMEM], out_specs=VMEM, compiler_params=grant,
        cost_estimate=cost(12 * modes * work, work),
    )(x, jnp.swapaxes(start_block, 1, 2))

    part, given = after(part, x)
    row = jnp.sum(swap(part, "chan"), axis=0)
    x = pl.pallas_call(
        transform_kernel,
        out_shape=split_shape, in_specs=[VMEM, VMEM], out_specs=VMEM, input_output_aliases={0: 0},
        compiler_params=grant, cost_estimate=cost(6 * waves * work, 6 * work),
    )(given, table)
    row, x = after(row, x)
    row = jnp.sum(to_all(row, "pix"), axis=0)
    grown = to_all(row, "chan")
    part = pl.pallas_call(
        lambda *refs: second_kernel(scale, modes, *refs),
        out_shape=share, in_specs=[VMEM, VMEM, VMEM], out_specs=VMEM, compiler_params=grant,
    )(x, grown, table)
    row = jnp.sum(swap(part, "chan"), axis=0)
    row = jnp.sum(to_all(row, "pix"), axis=0)
    grown = to_all(row, "chan")
    blocks = pl.pallas_call(
        lambda *refs: last_kernel(modes, *refs),
        out_shape=shape(owners, species, step // LANES, chans, LANES), in_specs=[VMEM, VMEM], out_specs=VMEM, compiler_params=grant,
        scratch_shapes=[pltpu.VMEM((species, owners, step // LANES, chans + 8, LANES), jnp.float32)],
    )(x, grown)
    return pl.pallas_call(
        join_kernel,
        out_shape=shape(2, species, waves // owners, pixels), in_specs=[VMEM], out_specs=HBM, compiler_params=params(8),
        scratch_shapes=[pltpu.VMEM((2, species, waves // owners, pixels), jnp.float32), DMA((2, species))],
    )(swap(blocks, "chan"))


def solution(mesh):
    placed = (P(None, "chan", "pix"), P())
    return jax.shard_map(
        body, mesh=mesh, in_specs=placed, out_specs=P(None, None, "chan", "pix"), check_vma=False
    )
```

```python
import jax
import jax.numpy as jnp
import numpy as np
from jax import lax
from jax.experimental import pallas as pl
from jax.experimental.pallas import tpu as pltpu
from jax.sharding import PartitionSpec as P

LANES = 128
GROUPS = 4
INNER, ROWS, OUTER = ((1,), (0,)), ((1,), (1,)), ((0,), (0,))
VMEM = pl.BlockSpec(memory_space=pltpu.VMEM)
HBM = pl.BlockSpec(memory_space=pltpu.HBM)
DMA = pltpu.SemaphoreType.DMA


def params(mib):
    return pltpu.CompilerParams(vmem_limit_bytes=mib * 1024 * 1024)


def swap(value, axis):
    return lax.all_to_all(value, axis, split_axis=0, concat_axis=0, tiled=True)


def to_all(value, axis):
    count = lax.axis_size(axis)
    return swap(jnp.broadcast_to(value[None], (count,) + value.shape), axis)


def after(value, others):
    return lax.optimization_barrier((value, others))


def cost(flops, moved):
    return pl.CostEstimate(flops=flops, bytes_accessed=moved, transcendentals=0)


def shape(*dims):
    return jax.ShapeDtypeStruct(dims, jnp.float32)


def dot(a, b, dims):
    return lax.dot_general(a, b, (dims, ((), ())), preferred_element_type=jnp.float32)


def cube_of(x_ref, s):
    parts, _, chans, pixels = x_ref.shape
    return x_ref[:, s].reshape(parts * chans, pixels)


def turned_cube(x_ref, s):
    owners, _, rows, pixels = x_ref.shape
    step = rows // GROUPS
    groups = [x_ref[:, s, q * step : (q + 1) * step].reshape(owners * step, pixels) for q in range(GROUPS)]
    return jnp.concatenate(groups, axis=0)


def store_turned(out_ref, value, s):
    owners, _, rows, pixels = out_ref.shape
    step = rows // GROUPS
    for q in range(GROUPS):
        part = value[q * owners * step : (q + 1) * owners * step]
        out_ref[:, s, q * step : (q + 1) * step] = part.reshape(owners, step, pixels)


def folded(value, axis):
    half = value.shape[axis] // 2
    first, second = lax.slice_in_dim(value, 0, half, axis=axis), lax.slice_in_dim(value, half, 2 * half, axis=axis)
    return first + second, first - second


def parts_of(value, count):
    parts = []
    for _ in range(count):
        part = value.astype(jnp.bfloat16)
        parts.append(part)
        value = value - part.astype(jnp.float32)
    return parts


def split_kernel(src, dst):
    step = dst.shape[3]
    for j in range(dst.shape[0]):
        dst[j] = src[:, :, j * step : (j + 1) * step]


def products_of_parts(left, right, dims):
    count = left[0].shape[0]
    stacked = jnp.concatenate(left, axis=0)
    a = dot(stacked, right[0], dims)
    b = dot(stacked[: 2 * count], right[1], dims)
    c = dot(stacked[:count], right[2], dims)
    return a[:count] + ((a[count : 2 * count] + b[:count]) + ((a[2 * count :] + b[count:]) + c))


def products(rows, right, dims):
    count = rows.shape[0]
    stacked = jnp.concatenate([part.astype(jnp.float32) for part in parts_of(rows, 3)], axis=0).astype(jnp.bfloat16)
    a = dot(stacked, right[0], dims)
    b = dot(stacked[: 2 * count], right[1], dims)
    c = dot(stacked[:count], right[2], dims)
    return a[:count] + ((a[count : 2 * count] + b[:count]) + ((a[2 * count :] + b[count:]) + c))


def expand(rows, weights):
    left = [part.astype(jnp.float32) for part in parts_of(rows, 3)]
    right = [part.astype(jnp.float32) for part in parts_of(weights, 3)]
    pairs = [(0, 0), (0, 1), (1, 0), (0, 2), (1, 1), (2, 0)]
    left = jnp.concatenate([left[a] for a, _ in pairs], axis=0).astype(jnp.bfloat16)
    right = jnp.concatenate([right[b] for _, b in pairs], axis=0).astype(jnp.bfloat16)
    return dot(left, right, OUTER)


def store_rows(out_ref, rows, s):
    modes = rows.shape[0]
    for c in range(rows.shape[1] // LANES):
        out_ref[s * modes : (s + 1) * modes, c, :] = rows[:, c * LANES : (c + 1) * LANES]


def grown_rows(g_ref, s, modes):
    return jnp.concatenate([g_ref[s * modes : (s + 1) * modes, c, :] for c in range(g_ref.shape[1])], axis=1)


def orthonormal(rows):
    modes = rows.shape[0]
    index = lax.broadcasted_iota(jnp.int32, (modes, 1), 0)
    for j in range(modes - 1):
        pivot = rows[j : j + 1]
        prods = jnp.sum(rows * pivot, axis=1, keepdims=True)
        ratio = jnp.where(index > j, prods / prods[j : j + 1], 0.0)
        rows = rows - ratio * pivot
    norms = jnp.sum(rows * rows, axis=1, keepdims=True)
    inverse = lax.rsqrt(norms)
    inverse = inverse * (1.5 - 0.5 * norms * inverse * inverse)
    return rows * inverse


def inverse_factor(rows):
    modes = rows.shape[0]
    index = lax.broadcasted_iota(jnp.int32, (modes, 1), 0)
    taken = lax.broadcasted_iota(jnp.int32, (modes, LANES), 0) == lax.broadcasted_iota(jnp.int32, (modes, LANES), 1)
    taken = taken.astype(jnp.float32)
    for j in range(modes - 1):
        pivot = rows[j : j + 1]
        prods = jnp.sum(rows * pivot, axis=1, keepdims=True)
        ratio = jnp.where(index > j, prods / prods[j : j + 1], 0.0)
        rows = rows - ratio * pivot
        taken = taken - ratio * taken[j : j + 1]
    norms = jnp.sum(rows * rows, axis=1, keepdims=True)
    inverse = lax.rsqrt(norms)
    inverse = inverse * (1.5 - 0.5 * norms * inverse * inverse)
    return taken * inverse


def mixed(factor, rows):
    total = factor[:, 0:1] * rows[0:1]
    for j in range(1, rows.shape[0]):
        total = total + factor[:, j : j + 1] * rows[j : j + 1]
    return total


def first_kernel(scale, x_ref, start_ref, out_ref):
    for s in range(x_ref.shape[1]):
        x_parts = parts_of(cube_of(x_ref, s), 3)
        weights = products(start_ref[s], x_parts, INNER) * scale
        store_rows(out_ref, products(weights, x_parts, ROWS), s)


def turned_rows(rows, table_ref):
    turned = [
        products(half, [table_ref[p, parity] for p in range(3)], ROWS) for parity, half in enumerate(folded(rows, 1))
    ]
    half = turned[0].shape[1] // 2
    return jnp.concatenate([turned[q % 2][:, q // 2 * half : (q // 2 + 1) * half] for q in range(GROUPS)], axis=1)


def transform_kernel(x_ref, table_ref, out_ref):
    for s in range(x_ref.shape[1]):
        halves = []
        for parity, x in enumerate(folded(cube_of(x_ref, s), 0)):
            halves.append(products_of_parts([table_ref[p, parity] for p in range(3)], parts_of(x, 3), INNER))
        half = halves[0].shape[0] // 2
        turned = [halves[q % 2][q // 2 * half : (q // 2 + 1) * half] for q in range(GROUPS)]
        store_turned(out_ref, jnp.concatenate(turned, axis=0), s)


def second_kernel(scale, modes, x_ref, g_ref, table_ref, out_ref):
    species = range(x_ref.shape[1])
    grown = [grown_rows(g_ref, s, modes) for s in species]
    turned = turned_rows(jnp.concatenate(grown, axis=0), table_ref)
    x_parts = [parts_of(turned_cube(x_ref, s), 3) for s in species]
    bases = [mixed(inverse_factor(grown[s]), turned[s * modes : (s + 1) * modes]) for s in species]
    weights = [products(basis, parts, INNER) * scale for basis, parts in zip(bases, x_parts)]
    for s in species:
        store_rows(out_ref, products(weights[s], x_parts[s], ROWS), s)


def last_kernel(modes, x_ref, g_ref, out_ref):
    owners, _, tiles, rows, _ = out_ref.shape
    count = rows // GROUPS
    species = range(x_ref.shape[1])
    bases = [orthonormal(grown_rows(g_ref, s, modes)) for s in species]
    cubes = [turned_cube(x_ref, s) for s in species]
    weights = [products(basis, parts_of(x, 3), INNER) for basis, x in zip(bases, cubes)]
    for s in species:
        fix = expand(bases[s], weights[s])
        cleaned = cubes[s] - fix
        scaled = cleaned * np.float32(np.sqrt(0.5))
        for q in range(GROUPS):
            rows = pl.ds(q // 2 * count * 2 + q % 2, count, stride=2)
            for c in range(tiles):
                part = scaled[q * owners * count : (q + 1) * owners * count, c * LANES : (c + 1) * LANES]
                out_ref[:, s, c, rows, :] = part.reshape(owners, count, LANES)
        for c in range(tiles):
            out_ref[0, s, c, 0:1, :] = cleaned[0:1, c * LANES : (c + 1) * LANES]
            out_ref[0, s, c, 2 * count : 2 * count + 1, :] = jnp.zeros((1, LANES), jnp.float32)


def join_kernel(src, dst, held, sems):
    halves, species, waves, _ = dst.shape
    copies = []
    for h in range(halves):
        for s in range(species):
            for j in range(src.shape[0]):
                for c in range(src.shape[2]):
                    at = (j * src.shape[2] + c) * LANES
                    held[h, s, :, at : at + LANES] = src[j, s, c, h * waves : (h + 1) * waves]
            copy = pltpu.make_async_copy(held.at[h, s], dst.at[h, s], sems.at[h, s])
            copy.start()
            copies.append(copy)
    for copy in copies:
        copy.wait()


def tables(owners, waves, width):
    k = np.arange(waves)[:, None]
    f = np.arange(width // 2)[None, :]
    phase = 2.0 * np.pi * (k * f % width) / width
    both = np.stack([np.cos(phase), -np.sin(phase)]) * np.sqrt(2.0 / width)
    both[0, 0] = 1.0 / np.sqrt(width)
    both[1, 0] = (1.0 - 2.0 * (f[0] % 2)) / np.sqrt(width)
    left = both.reshape(2, owners, waves // owners // 2, 2, width // 2).transpose(3, 0, 1, 2, 4).reshape(2, waves, width // 2)
    parts = []
    for _ in range(3):
        part = left.astype(jnp.bfloat16)
        parts.append(part)
        left = left - part.astype(np.float64)
    return np.stack(parts)


def body(cubes, start_block):
    owners = lax.axis_size("chan")
    species, chans, pixels = cubes.shape
    width = chans * owners
    modes = start_block.shape[2]
    waves = width // 2
    step = pixels // owners
    scale = 1.0 / (pixels * lax.axis_size("pix"))
    share = shape(species * modes, width // LANES, LANES)
    split_shape = shape(owners, species, chans, step)
    table = jnp.asarray(tables(owners, waves, width))
    work = 2 * species * width * step
    grant = params(24)

    split = pl.pallas_call(
        split_kernel,
        out_shape=split_shape, in_specs=[VMEM], out_specs=VMEM, compiler_params=params(4),
    )(cubes)
    x = swap(split, "chan")
    part = pl.pallas_call(
        lambda *refs: first_kernel(scale, *refs),
        out_shape=share, in_specs=[VMEM, VMEM], out_specs=VMEM, compiler_params=grant,
        cost_estimate=cost(12 * modes * work, work),
    )(x, jnp.swapaxes(start_block, 1, 2))

    part, given = after(part, x)
    row = jnp.sum(swap(part, "chan"), axis=0)
    x = pl.pallas_call(
        transform_kernel,
        out_shape=split_shape, in_specs=[VMEM, VMEM], out_specs=VMEM, input_output_aliases={0: 0},
        compiler_params=grant, cost_estimate=cost(6 * waves * work, 6 * work),
    )(given, table)
    row, x = after(row, x)
    row = jnp.sum(to_all(row, "pix"), axis=0)
    grown = to_all(row, "chan")
    part = pl.pallas_call(
        lambda *refs: second_kernel(scale, modes, *refs),
        out_shape=share, in_specs=[VMEM, VMEM, VMEM], out_specs=VMEM, compiler_params=grant,
    )(x, grown, table)
    row = jnp.sum(swap(part, "chan"), axis=0)
    row = jnp.sum(to_all(row, "pix"), axis=0)
    grown = to_all(row, "chan")
    blocks = pl.pallas_call(
        lambda *refs: last_kernel(modes, *refs),
        out_shape=shape(owners, species, step // LANES, chans, LANES), in_specs=[VMEM, VMEM], out_specs=VMEM, compiler_params=grant,
    )(x, grown)
    return pl.pallas_call(
        join_kernel,
        out_shape=shape(2, species, waves // owners, pixels), in_specs=[VMEM], out_specs=HBM, compiler_params=params(8),
        scratch_shapes=[pltpu.VMEM((2, species, waves // owners, pixels), jnp.float32), DMA((2, species))],
    )(swap(blocks, "chan"))


def solution(mesh):
    placed = (P(None, "chan", "pix"), P())
    return jax.shard_map(
        body, mesh=mesh, in_specs=placed, out_specs=P(None, None, "chan", "pix"), check_vma=False
    )
```

```python
import jax
import jax.numpy as jnp
import numpy as np
from jax import lax
from jax.experimental import pallas as pl
from jax.experimental.pallas import tpu as pltpu
from jax.sharding import PartitionSpec as P

LANES = 128
GROUPS = 4
INNER, ROWS, OUTER = ((1,), (0,)), ((1,), (1,)), ((0,), (0,))
VMEM = pl.BlockSpec(memory_space=pltpu.VMEM)
HBM = pl.BlockSpec(memory_space=pltpu.HBM)
DMA = pltpu.SemaphoreType.DMA


def params(mib):
    return pltpu.CompilerParams(vmem_limit_bytes=mib * 1024 * 1024)


def swap(value, axis):
    return lax.all_to_all(value, axis, split_axis=0, concat_axis=0, tiled=True)


def to_all(value, axis):
    count = lax.axis_size(axis)
    return swap(jnp.broadcast_to(value[None], (count,) + value.shape), axis)


def after(value, others):
    return lax.optimization_barrier((value, others))


def cost(flops, moved):
    return pl.CostEstimate(flops=flops, bytes_accessed=moved, transcendentals=0)


def shape(*dims):
    return jax.ShapeDtypeStruct(dims, jnp.float32)


def dot(a, b, dims):
    return lax.dot_general(a, b, (dims, ((), ())), preferred_element_type=jnp.float32)


def cube_of(x_ref, s):
    parts, _, chans, pixels = x_ref.shape
    return x_ref[:, s].reshape(parts * chans, pixels)


def turned_cube(x_ref, s):
    owners, _, rows, pixels = x_ref.shape
    step = rows // GROUPS
    groups = [x_ref[:, s, q * step : (q + 1) * step].reshape(owners * step, pixels) for q in range(GROUPS)]
    return jnp.concatenate(groups, axis=0)


def store_turned(out_ref, value, s):
    owners, _, rows, pixels = out_ref.shape
    step = rows // GROUPS
    for q in range(GROUPS):
        part = value[q * owners * step : (q + 1) * owners * step]
        out_ref[:, s, q * step : (q + 1) * step] = part.reshape(owners, step, pixels)


def folded(value, axis):
    half = value.shape[axis] // 2
    first, second = lax.slice_in_dim(value, 0, half, axis=axis), lax.slice_in_dim(value, half, 2 * half, axis=axis)
    return first + second, first - second


def parts_of(value, count):
    parts = []
    for _ in range(count):
        part = value.astype(jnp.bfloat16)
        parts.append(part)
        value = value - part.astype(jnp.float32)
    return parts


def split_kernel(src, dst):
    step = dst.shape[3]
    for j in range(dst.shape[0]):
        dst[j] = src[:, :, j * step : (j + 1) * step]


def products_of_parts(left, right, dims):
    count = left[0].shape[0]
    stacked = jnp.concatenate(left, axis=0)
    a = dot(stacked, right[0], dims)
    b = dot(stacked[: 2 * count], right[1], dims)
    c = dot(stacked[:count], right[2], dims)
    return a[:count] + ((a[count : 2 * count] + b[:count]) + ((a[2 * count :] + b[count:]) + c))


def products(rows, right, dims):
    count = rows.shape[0]
    stacked = jnp.concatenate([part.astype(jnp.float32) for part in parts_of(rows, 3)], axis=0).astype(jnp.bfloat16)
    a = dot(stacked, right[0], dims)
    b = dot(stacked[: 2 * count], right[1], dims)
    c = dot(stacked[:count], right[2], dims)
    return a[:count] + ((a[count : 2 * count] + b[:count]) + ((a[2 * count :] + b[count:]) + c))


def expand(rows, weights):
    left = [part.astype(jnp.float32) for part in parts_of(rows, 3)]
    right = [part.astype(jnp.float32) for part in parts_of(weights, 3)]
    pairs = [(0, 0), (0, 1), (1, 0), (0, 2), (1, 1), (2, 0)]
    left = jnp.concatenate([left[a] for a, _ in pairs], axis=0).astype(jnp.bfloat16)
    right = jnp.concatenate([right[b] for _, b in pairs], axis=0).astype(jnp.bfloat16)
    return dot(left, right, OUTER)


def store_rows(out_ref, rows, s):
    modes = rows.shape[0]
    for c in range(rows.shape[1] // LANES):
        out_ref[s * modes : (s + 1) * modes, c, :] = rows[:, c * LANES : (c + 1) * LANES]


def grown_rows(g_ref, s, modes):
    return jnp.concatenate([g_ref[s * modes : (s + 1) * modes, c, :] for c in range(g_ref.shape[1])], axis=1)


def orthonormal(rows):
    modes = rows.shape[0]
    index = lax.broadcasted_iota(jnp.int32, (modes, 1), 0)
    for j in range(modes - 1):
        pivot = rows[j : j + 1]
        prods = jnp.sum(rows * pivot, axis=1, keepdims=True)
        ratio = jnp.where(index > j, prods / prods[j : j + 1], 0.0)
        rows = rows - ratio * pivot
    norms = jnp.sum(rows * rows, axis=1, keepdims=True)
    inverse = lax.rsqrt(norms)
    inverse = inverse * (1.5 - 0.5 * norms * inverse * inverse)
    return rows * inverse


def inverse_factor(rows):
    modes = rows.shape[0]
    index = lax.broadcasted_iota(jnp.int32, (modes, 1), 0)
    taken = lax.broadcasted_iota(jnp.int32, (modes, LANES), 0) == lax.broadcasted_iota(jnp.int32, (modes, LANES), 1)
    taken = taken.astype(jnp.float32)
    for j in range(modes - 1):
        pivot = rows[j : j + 1]
        prods = jnp.sum(rows * pivot, axis=1, keepdims=True)
        ratio = jnp.where(index > j, prods / prods[j : j + 1], 0.0)
        rows = rows - ratio * pivot
        taken = taken - ratio * taken[j : j + 1]
    norms = jnp.sum(rows * rows, axis=1, keepdims=True)
    inverse = lax.rsqrt(norms)
    inverse = inverse * (1.5 - 0.5 * norms * inverse * inverse)
    return taken * inverse


def mixed(factor, rows):
    total = factor[:, 0:1] * rows[0:1]
    for j in range(1, rows.shape[0]):
        total = total + factor[:, j : j + 1] * rows[j : j + 1]
    return total


def first_kernel(scale, x_ref, start_ref, out_ref):
    for s in range(x_ref.shape[1]):
        x_parts = parts_of(cube_of(x_ref, s), 3)
        weights = products(start_ref[s], x_parts, INNER) * scale
        store_rows(out_ref, products(weights, x_parts, ROWS), s)


def turned_rows(rows, table_ref):
    turned = [
        products(half, [table_ref[p, parity] for p in range(3)], ROWS) for parity, half in enumerate(folded(rows, 1))
    ]
    half = turned[0].shape[1] // 2
    return jnp.concatenate([turned[q % 2][:, q // 2 * half : (q // 2 + 1) * half] for q in range(GROUPS)], axis=1)


def transform_kernel(x_ref, table_ref, out_ref):
    for s in range(x_ref.shape[1]):
        halves = []
        for parity, x in enumerate(folded(cube_of(x_ref, s), 0)):
            halves.append(products_of_parts([table_ref[p, parity] for p in range(3)], parts_of(x, 3), INNER))
        half = halves[0].shape[0] // 2
        turned = [halves[q % 2][q // 2 * half : (q // 2 + 1) * half] for q in range(GROUPS)]
        store_turned(out_ref, jnp.concatenate(turned, axis=0), s)


def second_kernel(scale, modes, x_ref, g_ref, table_ref, out_ref):
    species = range(x_ref.shape[1])
    grown = [grown_rows(g_ref, s, modes) for s in species]
    turned = turned_rows(jnp.concatenate(grown, axis=0), table_ref)
    x_parts = [parts_of(turned_cube(x_ref, s), 3) for s in species]
    bases = [mixed(inverse_factor(grown[s]), turned[s * modes : (s + 1) * modes]) for s in species]
    weights = [products(basis, parts, INNER) * scale for basis, parts in zip(bases, x_parts)]
    for s in species:
        store_rows(out_ref, products(weights[s], x_parts[s], ROWS), s)


def last_kernel(modes, x_ref, g_ref, out_ref, held):
    owners, _, tiles, rows, _ = out_ref.shape
    count = rows // GROUPS
    species = range(x_ref.shape[1])
    bases = [orthonormal(grown_rows(g_ref, s, modes)) for s in species]
    cubes = [turned_cube(x_ref, s) for s in species]
    weights = [products(basis, parts_of(x, 3), INNER) for basis, x in zip(bases, cubes)]
    for s in species:
        fix = expand(bases[s], weights[s])
        cleaned = cubes[s] - fix
        scaled = cleaned * np.float32(np.sqrt(0.5))
        for q in range(GROUPS):
            rows = pl.ds(q // 2 * count * 2 + q % 2, count, stride=2)
            for c in range(tiles):
                part = scaled[q * owners * count : (q + 1) * owners * count, c * LANES : (c + 1) * LANES]
                held[s, :, c, rows, :] = part.reshape(owners, count, LANES)
        out_ref[:, s] = held[s, :, :, : count * GROUPS]
        for c in range(tiles):
            out_ref[0, s, c, 0:1, :] = cleaned[0:1, c * LANES : (c + 1) * LANES]
            out_ref[0, s, c, 2 * count : 2 * count + 1, :] = jnp.zeros((1, LANES), jnp.float32)


def join_kernel(src, dst, held, sems):
    halves, species, waves, _ = dst.shape
    copies = []
    for h in range(halves):
        for s in range(species):
            for r in range(waves // 8):
                rows = pl.ds(r * 8, 8)
                for j in range(src.shape[0]):
                    for c in range(src.shape[2]):
                        at = (j * src.shape[2] + c) * LANES
                        first = h * waves + r * 8
                        held[h, s, r * 8 : (r + 1) * 8, at : at + LANES] = src[j, s, c, first : first + 8]
                copy = pltpu.make_async_copy(held.at[h, s, rows], dst.at[h, s, rows], sems.at[h, s, r])
                copy.start()
                copies.append(copy)
    for copy in copies:
        copy.wait()


def tables(owners, waves, width):
    k = np.arange(waves)[:, None]
    f = np.arange(width // 2)[None, :]
    phase = 2.0 * np.pi * (k * f % width) / width
    both = np.stack([np.cos(phase), -np.sin(phase)]) * np.sqrt(2.0 / width)
    both[0, 0] = 1.0 / np.sqrt(width)
    both[1, 0] = (1.0 - 2.0 * (f[0] % 2)) / np.sqrt(width)
    left = both.reshape(2, owners, waves // owners // 2, 2, width // 2).transpose(3, 0, 1, 2, 4).reshape(2, waves, width // 2)
    parts = []
    for _ in range(3):
        part = left.astype(jnp.bfloat16)
        parts.append(part)
        left = left - part.astype(np.float64)
    return np.stack(parts)


def body(cubes, start_block):
    owners = lax.axis_size("chan")
    species, chans, pixels = cubes.shape
    width = chans * owners
    modes = start_block.shape[2]
    waves = width // 2
    step = pixels // owners
    scale = 1.0 / (pixels * lax.axis_size("pix"))
    share = shape(species * modes, width // LANES, LANES)
    split_shape = shape(owners, species, chans, step)
    table = jnp.asarray(tables(owners, waves, width))
    work = 2 * species * width * step
    grant = params(24)

    split = pl.pallas_call(
        split_kernel,
        out_shape=split_shape, in_specs=[VMEM], out_specs=VMEM, compiler_params=params(4),
    )(cubes)
    x = swap(split, "chan")
    part = pl.pallas_call(
        lambda *refs: first_kernel(scale, *refs),
        out_shape=share, in_specs=[VMEM, VMEM], out_specs=VMEM, compiler_params=grant,
        cost_estimate=cost(12 * modes * work, work),
    )(x, jnp.swapaxes(start_block, 1, 2))

    part, given = after(part, x)
    row = jnp.sum(swap(part, "chan"), axis=0)
    x = pl.pallas_call(
        transform_kernel,
        out_shape=split_shape, in_specs=[VMEM, VMEM], out_specs=VMEM, input_output_aliases={0: 0},
        compiler_params=grant, cost_estimate=cost(6 * waves * work, 6 * work),
    )(given, table)
    row, x = after(row, x)
    row = jnp.sum(to_all(row, "pix"), axis=0)
    grown = to_all(row, "chan")
    part = pl.pallas_call(
        lambda *refs: second_kernel(scale, modes, *refs),
        out_shape=share, in_specs=[VMEM, VMEM, VMEM], out_specs=VMEM, compiler_params=grant,
    )(x, grown, table)
    row = jnp.sum(swap(part, "chan"), axis=0)
    row = jnp.sum(to_all(row, "pix"), axis=0)
    grown = to_all(row, "chan")
    blocks = pl.pallas_call(
        lambda *refs: last_kernel(modes, *refs),
        out_shape=shape(owners, species, step // LANES, chans, LANES), in_specs=[VMEM, VMEM], out_specs=VMEM, compiler_params=grant,
        scratch_shapes=[pltpu.VMEM((species, owners, step // LANES, chans + 8, LANES), jnp.float32)],
    )(x, grown)
    return pl.pallas_call(
        join_kernel,
        out_shape=shape(2, species, waves // owners, pixels), in_specs=[VMEM], out_specs=HBM, compiler_params=params(8),
        scratch_shapes=[pltpu.VMEM((2, species, waves // owners, pixels), jnp.float32), DMA((2, species, waves // owners // 8))],
    )(swap(blocks, "chan"))


def solution(mesh):
    placed = (P(None, "chan", "pix"), P())
    return jax.shard_map(
        body, mesh=mesh, in_specs=placed, out_specs=P(None, None, "chan", "pix"), check_vma=False
    )
```
